512 devices in a mesh: scen: 8 (over y), col: 64 (over z, x, core).
Axes of the slice: x: 4, y: 8, z: 8, core: 2. Of those that a mesh axis runs over, the one named last changes fastest.
Arguments:
- border: float32 [16, 1536, 16384], P('scen', None, 'col'), may hold values from -6 to 6
- barrier: float32 [16, 1536], P('scen'), may hold values from 0.1 to 10
- row_counts: int32 [16], P('scen'), may hold values from 1024 to 1536, as said below
Outputs:
- factor_panel: float32 [64, 8, 32, 512], P('col', 'scen')
The draws below stay inside these ranges and needn't reach their ends.
Inputs may be any that keep to these rules, and one draw needn't show every extreme that they name: `row_counts`: every value lies between 1024 and 1536, and at least one scenario uses all 1536 rows.
All inputs are finite; a program needn't handle non-finite values.
Results may differ from the reference program's by a relative error of at most 0.0003.
Values sent between devices are 32-bit elements; how exact they have to be, the bound alone decides.
No kernel may reach another device: no remote copies, remote signals or barrier semaphores. Data moves between devices by JAX's collectives and lax.ppermute only.
A program may use at most 64 MiB of HBM per device.

```python
import math
import jax
import jax.numpy as jnp
from jax import lax

NB = 16384
PANEL = 512
RMAX = 1536
SCEN = 16
N_SCEN = 8
N_COL = 64


def draw_row_counts(key, part):
    counts = jax.random.randint(jax.random.fold_in(key, 11), (SCEN,), 2 * RMAX // 3, RMAX + 1)
    chosen = jax.random.randint(jax.random.fold_in(key, 23), (), 0, SCEN)
    return jnp.where(jnp.arange(SCEN) == chosen, RMAX, counts).astype(jnp.int32)


def block_levels(key, dims, cuts, smallest, high):
    gain = 1.0
    for position, parts in cuts:
        steps = jax.random.uniform(jax.random.fold_in(jax.random.fold_in(key, 6), position), (parts,), jnp.float32, smallest / len(cuts), high / len(cuts))
        gain = gain * jnp.repeat(jnp.exp(steps), dims[position] // parts).reshape((-1,) + (1,) * (len(dims) - 1 - position))
    return gain


def gaussian(key, extent, scale, reach, pieces=(), held_as=jnp.bfloat16):
    result = jax.random.normal(key, extent, jnp.float32) * scale
    if len(pieces) > 0:
        result = block_levels(key, extent, pieces, -0.22, 0.18) * result
    return jnp.clip(result, min=-reach, max=reach).astype(held_as)


def setup_inputs(seed: int = 0) -> dict:
    key_of = jax.random.split(jax.random.key(seed), 4)
    return {
        "border": gaussian(key_of[0], (SCEN, RMAX, NB), 1.0, 6.0, ((0, 8), (2, 64)), jnp.float32),
        "barrier": jnp.clip(jnp.exp(math.log(10.0) - 4.6051702 * jax.random.uniform(key_of[1], (SCEN, RMAX), jnp.float32) ** block_levels(key_of[1], (SCEN, RMAX), ((0, 8),), -0.2, 0.2)), 0.1, 10.0),
        "row_counts": draw_row_counts(jax.random.fold_in(key_of[3], 71), 0),
    }


def reference(border, barrier, row_counts):
    positions = lax.iota(jnp.int32, RMAX)
    weights = jnp.where(positions[None, :] < row_counts[:, None], 1.0 / barrier, jnp.float32(0.0))
    split_cols = border.reshape(SCEN, RMAX, N_COL, NB // N_COL)
    panel_border = split_cols[:, :, :, :PANEL // N_COL].reshape(SCEN, RMAX, PANEL)

    def accumulate(carry, items):
        border_one, weight_one, panel_one = items
        weighted = border_one * weight_one[:, None]
        term = jnp.einsum('rc,rk->ck', weighted.astype(jnp.float32), panel_one.astype(jnp.float32), precision=lax.Precision.HIGHEST, preferred_element_type=jnp.float32)
        return (carry + term, None)
    schur, _ = lax.scan(accumulate, jnp.zeros((NB, PANEL), jnp.float32), (border, weights, panel_border))
    block = schur.reshape(N_COL, NB // N_COL, PANEL)[:, :PANEL // N_COL, :].reshape(PANEL, PANEL)
    lower = jnp.linalg.cholesky(block)
    solved = lax.linalg.triangular_solve(lower, schur, left_side=False, lower=True, transpose_a=True)
    return solved.reshape(N_COL, N_SCEN, NB // (N_COL * N_SCEN), PANEL)
```

```python
import jax
import jax.numpy as jnp
from jax import lax
from jax.experimental import pallas as pl
from jax.experimental.pallas import tpu as pltpu
from jax.sharding import Mesh, PartitionSpec as P

PANEL = 512
BLOCK = 128
TILE = 8
COL = ("z", "x", "core")
SWAP = [(0, 1), (1, 0)]


def dot(a, b, dim_a, dim_b):
    return lax.dot_general(
        a, b, (((dim_a,), (dim_b,)), ((), ())),
        precision=lax.Precision.HIGHEST, preferred_element_type=jnp.float32,
    )


def factor_inverse(diagonal):
    count = BLOCK // TILE
    row_of = lax.broadcasted_iota(jnp.int32, (TILE, BLOCK), 0)
    col_of = lax.broadcasted_iota(jnp.int32, (TILE, BLOCK), 1)
    below = lax.broadcasted_iota(jnp.int32, (TILE, 1), 0)
    left = [diagonal[TILE * t:TILE * (t + 1), :] for t in range(count)]
    right = [jnp.where(col_of == row_of + TILE * t, jnp.float32(1.0), jnp.float32(0.0)) for t in range(count)]
    for j in range(BLOCK):
        first, r = divmod(j, TILE)
        row = left[first][r:r + 1, :]
        scale = 1.0 / row[:, j:j + 1]
        row_left = row * scale
        row_right = right[first][r:r + 1, :] * scale
        for t in range(first, count):
            if t == first and r == TILE - 1:
                continue
            factor = left[t][:, j:j + 1]
            if t == first:
                factor = jnp.where(below > r, factor, 0.0)
            left[t] = left[t] - factor * row_left
            right[t] = right[t] - factor * row_right
    rows = []
    for t in range(count):
        pivots = jnp.sum(jnp.where(col_of == row_of + TILE * t, left[t], 0.0), axis=1, keepdims=True)
        rows.append(right[t] * lax.rsqrt(pivots))
    return jnp.concatenate(rows, axis=0)


def inverse_kernel(block_ref, out_ref, rest, sums):
    rest[...] = block_ref[...]
    sums[...] = jnp.zeros_like(sums)
    out_ref[...] = jnp.zeros_like(out_ref)
    for a in range(0, PANEL, BLOCK):
        b = a + BLOCK
        inverse = factor_inverse(rest[a:b, a:b])
        out_ref[a:b, a:b] = inverse
        if a > 0:
            out_ref[a:b, 0:a] = -dot(inverse, sums[a:b, 0:a], 1, 0)
        if b < PANEL:
            upper = dot(inverse, rest[a:b, b:PANEL], 1, 0)
            rest[b:PANEL, b:PANEL] = rest[b:PANEL, b:PANEL] - dot(upper, upper, 0, 0)
            sums[b:PANEL, 0:b] = sums[b:PANEL, 0:b] + dot(upper, out_ref[a:b, 0:b], 0, 0)


def inverse_factor(block):
    shape = (PANEL, PANEL)
    return pl.pallas_call(
        inverse_kernel,
        out_shape=jax.ShapeDtypeStruct(shape, jnp.float32),
        in_specs=[pl.BlockSpec(memory_space=pltpu.VMEM)],
        out_specs=pl.BlockSpec(memory_space=pltpu.VMEM),
        scratch_shapes=[pltpu.VMEM(shape, jnp.float32), pltpu.VMEM(shape, jnp.float32)],
        compiler_params=pltpu.CompilerParams(vmem_limit_bytes=32 << 20),
        cost_estimate=pl.CostEstimate(flops=4 * PANEL ** 3, bytes_accessed=8 * PANEL ** 2, transcendentals=PANEL),
        name="inverse_factor",
    )(block)


def product(weighted, panel):
    return jnp.einsum(
        "rc,kr->ck", weighted, panel,
        precision=lax.Precision.HIGH, preferred_element_type=jnp.float32,
    )


def body(border, barrier, row_counts):
    capacity = border.shape[1]
    own_cols = border.shape[2]
    n_scen = lax.axis_size("scen")
    n_x = lax.axis_size("x")
    n_z = lax.axis_size("z")
    per_owner = PANEL // (n_z * n_x * 2)
    rows_owned = own_cols // n_scen
    core = lax.axis_index("core")

    panel_part = jnp.transpose(border[:, :, :per_owner], (0, 2, 1))
    to_send = jnp.broadcast_to(panel_part[None], (n_x, 2, per_owner, capacity))
    beside = lax.all_to_all(
        to_send.reshape(n_x * 2, per_owner, capacity), ("x", "core"), split_axis=0, concat_axis=0, tiled=True
    ).reshape(n_x * 2 * per_owner, capacity)
    panel = lax.all_gather(beside, "z", axis=0, tiled=True)

    positions = lax.iota(jnp.int32, capacity)
    here = lax.dynamic_index_in_dim(barrier, core, 0, keepdims=False)
    count = lax.dynamic_index_in_dim(row_counts, core, 0, keepdims=False)
    weights = jnp.where(positions < count, 1.0 / here, jnp.float32(0.0))

    mine = lax.dynamic_index_in_dim(border, core, 0, keepdims=False)
    other = lax.ppermute(lax.dynamic_index_in_dim(border, 1 - core, 0, keepdims=False), "core", SWAP)

    chip_rows = lax.dynamic_slice_in_dim(beside, lax.axis_index("x") * 2 * per_owner, 2 * per_owner, 0)
    block_part = jnp.einsum(
        "ir,kr->ik", chip_rows * weights[None, :], panel,
        precision=lax.Precision.HIGHEST, preferred_element_type=jnp.float32,
    )
    parts = jnp.broadcast_to(block_part.reshape(1, 2, per_owner, PANEL), (n_scen, 2, per_owner, PANEL))
    parts = lax.all_to_all(
        parts.reshape(n_scen * 2, per_owner, PANEL), ("scen", "core"), split_axis=0, concat_axis=0, tiled=True
    )
    summed_rows = jnp.sum(parts, axis=0)
    copies = jnp.broadcast_to(summed_rows, (PANEL // per_owner, per_owner, PANEL))
    block = lax.all_to_all(copies, COL, split_axis=0, concat_axis=0, tiled=True).reshape(PANEL, PANEL)
    inverse = inverse_factor(block)

    schur_mine = product(mine * weights[:, None], panel)
    schur_other = product(other * weights[:, None], panel)
    schur_part = schur_mine + lax.ppermute(schur_other, "core", SWAP)
    owned = lax.psum_scatter(schur_part, "scen", scatter_dimension=0, tiled=True)
    solved = dot(owned, inverse, 1, 1)
    return solved.reshape(1, 1, rows_owned, PANEL)


def solution(mesh):
    inner = Mesh(mesh.devices.reshape(mesh.shape["scen"], 8, 4, 2), ("scen",) + COL)
    placed = (P("scen", None, COL), P("scen", None), P("scen"))
    return jax.shard_map(
        body, mesh=inner, in_specs=placed, out_specs=P(COL, "scen", None, None), check_vma=False
    )
```

```python
import jax
import jax.numpy as jnp
from jax import lax
from jax.experimental import pallas as pl
from jax.experimental.pallas import tpu as pltpu
from jax.sharding import Mesh, PartitionSpec as P

PANEL = 512
BLOCK = 128
TILE = 8
COL = ("z", "x", "core")
SWAP = [(0, 1), (1, 0)]


def dot(a, b, dim_a, dim_b):
    return lax.dot_general(
        a, b, (((dim_a,), (dim_b,)), ((), ())),
        precision=lax.Precision.HIGHEST, preferred_element_type=jnp.float32,
    )


def reciprocal(x):
    first = pltpu.reciprocal(x, approx=True)
    return first * (2.0 - x * first)


def spread(piece):
    return jnp.broadcast_to(piece, (TILE, BLOCK))


def factor_inverse(diagonal):
    count = BLOCK // TILE
    row_of = lax.broadcasted_iota(jnp.int32, (TILE, BLOCK), 0)
    col_of = lax.broadcasted_iota(jnp.int32, (TILE, BLOCK), 1)
    left = [diagonal[TILE * t:TILE * (t + 1), :] for t in range(count)]
    right = [jnp.where(col_of == row_of + TILE * t, jnp.float32(1.0), jnp.float32(0.0)) for t in range(count)]
    rows = []
    for s in range(count):
        own = [spread(left[s][:, TILE * s + c:TILE * s + c + 1]) for c in range(TILE)]
        rest = [[spread(own[c][r:r + 1, :]) for c in range(r + 1)] for r in range(TILE)]
        up_left = [spread(left[s][r:r + 1, :]) for r in range(TILE)]
        up_right = [spread(right[s][r:r + 1, :]) for r in range(TILE)]
        inverse = [None] * TILE
        factor = [[None] * TILE for _ in range(TILE)]
        for c in range(TILE):
            inverse[c] = reciprocal(rest[c][c])
            for r in range(c + 1, TILE):
                factor[r][c] = rest[r][c] * inverse[c]
            for r in range(c + 1, TILE):
                for q in range(c + 1, r + 1):
                    rest[r][q] = rest[r][q] - factor[r][c] * rest[q][c]
                up_left[r] = up_left[r] - factor[r][c] * up_left[c]
                up_right[r] = up_right[r] - factor[r][c] * up_right[c]
        if s < count - 1:
            down_left = [None] * TILE
            down_right = [None] * TILE
            for c in range(TILE - 1, -1, -1):
                down_left[c] = inverse[c] * up_left[c]
                down_right[c] = inverse[c] * up_right[c]
                for r in range(c + 1, TILE):
                    down_left[c] = down_left[c] - factor[r][c] * down_left[r]
                    down_right[c] = down_right[c] - factor[r][c] * down_right[r]
            for t in range(s + 1, count):
                across = [spread(left[t][:, TILE * s + c:TILE * s + c + 1]) for c in range(TILE)]
                for c in range(TILE - 1, -1, -1):
                    left[t] = left[t] - across[c] * down_left[c]
                    right[t] = right[t] - across[c] * down_right[c]
        scaled = lax.rsqrt(rest[0][0]) * up_right[0]
        for r in range(1, TILE):
            scaled = jnp.where(row_of == r, lax.rsqrt(rest[r][r]) * up_right[r], scaled)
        rows.append(scaled)
    return jnp.concatenate(rows, axis=0)


def inverse_kernel(core_ref, own_ref, other_ref, out_ref, rest, sums):
    core = core_ref[0]
    for half_ref, half in ((own_ref, core), (other_ref, 1 - core)):
        for x in range(4):
            for k in range(2):
                for pair in range(4):
                    one = half_ref[8 * pair + x, 16 * k:16 * (k + 1), :]
                    two = half_ref[8 * pair + 4 + x, 16 * k:16 * (k + 1), :]
                    for h in range(2):
                        at = pl.multiple_of(half * 256, 256) + h * 128 + k * 64 + x * 16
                        rest[pl.ds(at, 16), pl.ds(128 * pair, 128)] = jnp.concatenate(
                            [one[:, 64 * h:64 * (h + 1)], two[:, 64 * h:64 * (h + 1)]], axis=1
                        )
    sums[...] = jnp.zeros_like(sums)
    out_ref[...] = jnp.zeros_like(out_ref)
    for a in range(0, PANEL, BLOCK):
        b = a + BLOCK
        inverse = factor_inverse(rest[a:b, a:b])
        out_ref[a:b, a:b] = inverse
        if a > 0:
            out_ref[a:b, 0:a] = -dot(inverse, sums[a:b, 0:a], 1, 0)
        if b < PANEL:
            upper = dot(inverse, rest[a:b, b:PANEL], 1, 0)
            rest[b:PANEL, b:PANEL] = rest[b:PANEL, b:PANEL] - dot(upper, upper, 0, 0)
            sums[b:PANEL, 0:b] = sums[b:PANEL, 0:b] + dot(upper, out_ref[a:b, 0:b], 0, 0)


def inverse_factor(core, own, other):
    shape = (PANEL, PANEL)
    return pl.pallas_call(
        inverse_kernel,
        out_shape=jax.ShapeDtypeStruct(shape, jnp.float32),
        in_specs=[pl.BlockSpec(memory_space=pltpu.SMEM)] + [pl.BlockSpec(memory_space=pltpu.VMEM)] * 2,
        out_specs=pl.BlockSpec(memory_space=pltpu.VMEM),
        scratch_shapes=[pltpu.VMEM(shape, jnp.float32), pltpu.VMEM(shape, jnp.float32)],
        compiler_params=pltpu.CompilerParams(vmem_limit_bytes=32 << 20),
        cost_estimate=pl.CostEstimate(flops=4 * PANEL ** 3, bytes_accessed=8 * PANEL ** 2, transcendentals=PANEL),
        name="inverse_factor",
    )(core, own, other)


def product(weighted, panel):
    return jnp.einsum(
        "rc,kr->ck", weighted, panel,
        precision=lax.Precision.HIGH, preferred_element_type=jnp.float32,
    )


def body(border, barrier, row_counts):
    capacity = border.shape[1]
    own_cols = border.shape[2]
    n_scen = lax.axis_size("scen")
    n_x = lax.axis_size("x")
    n_z = lax.axis_size("z")
    per_owner = PANEL // (n_z * n_x * 2)
    rows_owned = own_cols // n_scen
    core = lax.axis_index("core")

    panel_part = jnp.transpose(border[:, :, :per_owner], (0, 2, 1))
    to_send = jnp.broadcast_to(panel_part[None], (n_x, 2, per_owner, capacity))
    beside = lax.all_to_all(
        to_send.reshape(n_x * 2, per_owner, capacity), ("x", "core"), split_axis=0, concat_axis=0, tiled=True
    ).reshape(n_x * 2 * per_owner, capacity)
    panel = lax.all_gather(beside, "z", axis=0, tiled=True)

    positions = lax.iota(jnp.int32, capacity)
    here = lax.dynamic_index_in_dim(barrier, core, 0, keepdims=False)
    count = lax.dynamic_index_in_dim(row_counts, core, 0, keepdims=False)
    weights = jnp.where(positions < count, 1.0 / here, jnp.float32(0.0))

    mine = lax.dynamic_index_in_dim(border, core, 0, keepdims=False)
    other = lax.ppermute(lax.dynamic_index_in_dim(border, 1 - core, 0, keepdims=False), "core", SWAP)

    chip_rows = lax.dynamic_slice_in_dim(beside, lax.axis_index("x") * 2 * per_owner, 2 * per_owner, 0)
    along = lax.all_gather(chip_rows, "z", axis=0, tiled=True)
    block_part = jnp.einsum(
        "qr,pr->qp", along, beside * weights[None, :],
        precision=lax.Precision.HIGHEST, preferred_element_type=jnp.float32,
    )
    halves = block_part.reshape(2, 2, 4 * per_owner, 8 * per_owner)
    halves = jnp.concatenate([halves[:, 0], halves[:, 1]], axis=-1)
    part = halves.shape[1:]
    parts = jnp.broadcast_to(halves[None], (n_scen, 2) + part).reshape((n_scen * 2,) + part)
    parts = lax.all_to_all(parts, ("scen", "core"), split_axis=0, concat_axis=0, tiled=True)
    copies = jnp.broadcast_to(jnp.sum(parts, axis=0), (n_z * n_x,) + part)
    own_half = lax.all_to_all(copies, ("z", "x"), split_axis=0, concat_axis=0, tiled=True)
    other_half = lax.ppermute(own_half, "core", SWAP)
    inverse = inverse_factor(jnp.reshape(core, (1,)), own_half, other_half)

    schur_mine = product(mine * weights[:, None], panel)
    schur_other = product(other * weights[:, None], panel)
    schur_part = schur_mine + lax.ppermute(schur_other, "core", SWAP)
    owned = lax.psum_scatter(schur_part, "scen", scatter_dimension=0, tiled=True)
    solved = dot(owned, inverse, 1, 1)
    return solved.reshape(1, 1, rows_owned, PANEL)


def solution(mesh):
    inner = Mesh(mesh.devices.reshape(mesh.shape["scen"], 8, 4, 2), ("scen",) + COL)
    placed = (P("scen", None, COL), P("scen", None), P("scen"))
    return jax.shard_map(
        body, mesh=inner, in_specs=placed, out_specs=P(COL, "scen", None, None), check_vma=False
    )
```

```python
import jax
import jax.numpy as jnp
from jax import lax
from jax.experimental import pallas as pl
from jax.experimental.pallas import tpu as pltpu
from jax.sharding import Mesh, PartitionSpec as P

PANEL = 512
BLOCK = 128
TILE = 8
COL = ("z", "x", "core")
SWAP = [(0, 1), (1, 0)]


def dot(a, b, dim_a, dim_b):
    return lax.dot_general(
        a, b, (((dim_a,), (dim_b,)), ((), ())),
        precision=lax.Precision.HIGHEST, preferred_element_type=jnp.float32,
    )


def reciprocal(x):
    first = pltpu.reciprocal(x, approx=True)
    return first * (2.0 - x * first)


def spread(piece):
    return jnp.broadcast_to(piece, (TILE, BLOCK))


def factor_inverse(diagonal):
    count = BLOCK // TILE
    row_of = lax.broadcasted_iota(jnp.int32, (TILE, BLOCK), 0)
    col_of = lax.broadcasted_iota(jnp.int32, (TILE, BLOCK), 1)
    left = [diagonal[TILE * t:TILE * (t + 1), :] for t in range(count)]
    right = [jnp.where(col_of == row_of + TILE * t, jnp.float32(1.0), jnp.float32(0.0)) for t in range(count)]
    rows = []
    for s in range(count):
        own = [spread(left[s][:, TILE * s + c:TILE * s + c + 1]) for c in range(TILE)]
        rest = [[spread(own[c][r:r + 1, :]) for c in range(r + 1)] for r in range(TILE)]
        up_left = [spread(left[s][r:r + 1, :]) for r in range(TILE)]
        up_right = [spread(right[s][r:r + 1, :]) for r in range(TILE)]
        inverse = [None] * TILE
        factor = [[None] * TILE for _ in range(TILE)]
        for c in range(TILE):
            inverse[c] = reciprocal(rest[c][c])
            for r in range(c + 1, TILE):
                factor[r][c] = rest[r][c] * inverse[c]
            for r in range(c + 1, TILE):
                for q in range(c + 1, r + 1):
                    rest[r][q] = rest[r][q] - factor[r][c] * rest[q][c]
                up_left[r] = up_left[r] - factor[r][c] * up_left[c]
                up_right[r] = up_right[r] - factor[r][c] * up_right[c]
        if s < count - 1:
            down_left = [None] * TILE
            down_right = [None] * TILE
            for c in range(TILE - 1, -1, -1):
                down_left[c] = inverse[c] * up_left[c]
                down_right[c] = inverse[c] * up_right[c]
                for r in range(c + 1, TILE):
                    down_left[c] = down_left[c] - factor[r][c] * down_left[r]
                    down_right[c] = down_right[c] - factor[r][c] * down_right[r]
            for t in range(s + 1, count):
                across = [spread(left[t][:, TILE * s + c:TILE * s + c + 1]) for c in range(TILE)]
                for c in range(TILE - 1, -1, -1):
                    left[t] = left[t] - across[c] * down_left[c]
                    right[t] = right[t] - across[c] * down_right[c]
        scaled = lax.rsqrt(rest[0][0]) * up_right[0]
        for r in range(1, TILE):
            scaled = jnp.where(row_of == r, lax.rsqrt(rest[r][r]) * up_right[r], scaled)
        rows.append(scaled)
    return jnp.concatenate(rows, axis=0)


def inverse_kernel(core_ref, own_ref, other_ref, out_ref, rest, sums, lower):
    core = core_ref[0]
    for half_ref, half in ((own_ref, core), (other_ref, 1 - core)):
        for x in range(4):
            for k in range(2):
                for pair in range(4):
                    one = half_ref[8 * pair + x, 16 * k:16 * (k + 1), :]
                    two = half_ref[8 * pair + 4 + x, 16 * k:16 * (k + 1), :]
                    for h in range(2):
                        at = pl.multiple_of(half * 256, 256) + h * 128 + k * 64 + x * 16
                        rest[pl.ds(at, 16), pl.ds(128 * pair, 128)] = jnp.concatenate(
                            [one[:, 64 * h:64 * (h + 1)], two[:, 64 * h:64 * (h + 1)]], axis=1
                        )
    sums[...] = jnp.zeros_like(sums)
    lower[...] = jnp.zeros_like(lower)
    for a in range(0, PANEL, BLOCK):
        b = a + BLOCK
        inverse = factor_inverse(rest[a:b, a:b])
        lower[a:b, a:b] = inverse
        if a > 0:
            lower[a:b, 0:a] = -dot(inverse, sums[a:b, 0:a], 1, 0)
        if b < PANEL:
            upper = dot(inverse, rest[a:b, b:PANEL], 1, 0)
            rest[b:PANEL, b:PANEL] = rest[b:PANEL, b:PANEL] - dot(upper, upper, 0, 0)
            sums[b:PANEL, 0:b] = sums[b:PANEL, 0:b] + dot(upper, lower[a:b, 0:b], 0, 0)
    for k in range(0, PANEL, BLOCK):
        for a in range(0, PANEL, BLOCK):
            turned = jnp.transpose(lower[a:a + BLOCK, k:k + BLOCK]) if a >= k else jnp.zeros((BLOCK, BLOCK), jnp.float32)
            for piece in range(0, BLOCK, 16):
                z, x = divmod((k + piece) // 16, 4)
                to = 128 * x + 16 * z
                out_ref[to:to + 16, a:a + BLOCK] = turned[piece:piece + 16, :]


def inverse_factor(core, own, other):
    shape = (PANEL, PANEL)
    return pl.pallas_call(
        inverse_kernel,
        out_shape=jax.ShapeDtypeStruct(shape, jnp.float32),
        in_specs=[pl.BlockSpec(memory_space=pltpu.SMEM)] + [pl.BlockSpec(memory_space=pltpu.VMEM)] * 2,
        out_specs=pl.BlockSpec(memory_space=pltpu.VMEM),
        scratch_shapes=[pltpu.VMEM(shape, jnp.float32)] * 3,
        compiler_params=pltpu.CompilerParams(vmem_limit_bytes=16 << 20),
        cost_estimate=pl.CostEstimate(flops=4 * PANEL ** 3, bytes_accessed=8 * PANEL ** 2, transcendentals=PANEL),
        name="inverse_factor",
    )(core, own, other)


def prepare_kernel(counts_ref, barrier_ref, border_ref, along_ref, beside_ref, columns, arrived):
    capacity = barrier_ref.shape[1]
    copies = [
        pltpu.make_async_copy(border_ref.at[s, :, pl.ds(0, 128)], columns.at[s], arrived.at[s]) for s in range(2)
    ]
    for copy in copies:
        copy.start()
    position = lax.broadcasted_iota(jnp.int32, (1, capacity), 1)
    for s in range(2):
        weights = jnp.where(position < counts_ref[s], 1.0 / barrier_ref[s:s + 1, :], 0.0)
        copies[s].wait()
        tiles = [jnp.transpose(columns[s, a:a + 128, :])[:TILE, :] for a in range(0, capacity, 128)]
        panel = jnp.concatenate(tiles, axis=1)
        weighted = panel * weights
        for z in range(8):
            along_ref[2 * z + s] = weighted
        for x in range(4):
            beside_ref[2 * x + s] = panel


def prepare(row_counts, barrier, border):
    capacity = border.shape[1]
    vmem = pl.BlockSpec(memory_space=pltpu.VMEM)
    return pl.pallas_call(
        prepare_kernel,
        out_shape=(
            jax.ShapeDtypeStruct((16, TILE, capacity), jnp.float32),
            jax.ShapeDtypeStruct((8, TILE, capacity), jnp.float32),
        ),
        in_specs=[pl.BlockSpec(memory_space=pltpu.SMEM), vmem, pl.BlockSpec(memory_space=pltpu.HBM)],
        out_specs=(vmem, vmem),
        scratch_shapes=[pltpu.VMEM((2, capacity, 128), jnp.float32), pltpu.SemaphoreType.DMA((2,))],
        compiler_params=pltpu.CompilerParams(vmem_limit_bytes=60 << 20),
        name="prepare",
    )(row_counts, barrier, border)


def block_kernel(along_ref, beside_ref, out_ref):
    along = along_ref[...].reshape(16 * TILE, -1)
    beside = beside_ref[...].reshape(8 * TILE, -1)
    part = dot(along, beside, 1, 1)
    quarter = 4 * TILE
    for c in range(2):
        first = part[2 * c * quarter:(2 * c + 1) * quarter]
        second = part[(2 * c + 1) * quarter:(2 * c + 2) * quarter]
        packed = jnp.concatenate([first, second], axis=1)
        for y in range(8):
            out_ref[2 * y + c] = packed


def block_part(along, beside):
    vmem = pl.BlockSpec(memory_space=pltpu.VMEM)
    return pl.pallas_call(
        block_kernel,
        out_shape=jax.ShapeDtypeStruct((16, 4 * TILE, 16 * TILE), jnp.float32),
        in_specs=[vmem, vmem],
        out_specs=vmem,
        compiler_params=pltpu.CompilerParams(vmem_limit_bytes=16 << 20),
        name="block_part",
    )(along, beside)


def product(columns, panel):
    return jnp.einsum(
        "rc,kr->ck", columns, panel,
        precision=lax.Precision.HIGH, preferred_element_type=jnp.float32,
    )


def exchange(array, axes):
    return lax.all_to_all(array, axes, split_axis=0, concat_axis=0, tiled=True)


def body(border, barrier, row_counts):
    capacity = border.shape[1]
    own_cols = border.shape[2]
    n_scen = lax.axis_size("scen")
    rows_owned = own_cols // n_scen
    core = lax.axis_index("core")

    to_along, to_beside = prepare(row_counts, barrier, border)
    along = exchange(to_along, ("z", "core"))
    panel = lax.all_gather(along.reshape(16 * TILE, capacity), "x", axis=0, tiled=True)

    beside = exchange(to_beside, ("x", "core"))
    piece = block_part(along, beside)
    parts = exchange(piece, ("scen", "core"))
    copies = jnp.broadcast_to(jnp.sum(parts, axis=0), (32,) + parts.shape[1:])
    own_half = exchange(copies, ("z", "x"))
    other_half = lax.ppermute(own_half, "core", SWAP)
    inverse = inverse_factor(jnp.reshape(core, (1,)), own_half, other_half)

    border, _ = lax.optimization_barrier((border, piece))
    mine = lax.dynamic_index_in_dim(border, core, 0, keepdims=False)
    other = lax.ppermute(lax.dynamic_index_in_dim(border, 1 - core, 0, keepdims=False), "core", SWAP)
    schur_other = product(other, panel)
    schur_mine = product(mine, panel)
    schur_part = schur_mine + lax.ppermute(schur_other, "core", SWAP)
    owned = lax.psum_scatter(schur_part, "scen", scatter_dimension=0, tiled=True)
    solved = dot(owned, inverse, 1, 0)
    return solved.reshape(1, 1, rows_owned, PANEL)


def solution(mesh):
    inner = Mesh(mesh.devices.reshape(mesh.shape["scen"], 8, 4, 2), ("scen",) + COL)
    placed = (P("scen", None, COL), P("scen", None), P("scen"))
    return jax.shard_map(
        body, mesh=inner, in_specs=placed, out_specs=P(COL, "scen", None, None), check_vma=False
    )
```

```python
import jax
import jax.numpy as jnp
from jax import lax
from jax.experimental import pallas as pl
from jax.experimental.pallas import tpu as pltpu
from jax.sharding import Mesh, PartitionSpec as P

PANEL = 512
BLOCK = 128
TILE = 8
COL = ("z", "x", "core")
SWAP = [(0, 1), (1, 0)]


def dot(a, b, dim_a, dim_b):
    return lax.dot_general(
        a, b, (((dim_a,), (dim_b,)), ((), ())),
        precision=lax.Precision.HIGHEST, preferred_element_type=jnp.float32,
    )


def reciprocal(x):
    return pltpu.reciprocal(x, approx=True)


def spread(piece):
    return jnp.broadcast_to(piece, (TILE, BLOCK))


def rows_of(values):
    row_of = lax.broadcasted_iota(jnp.int32, (TILE, BLOCK), 0)
    tile = values[0]
    for r in range(1, TILE):
        tile = jnp.where(row_of == r, values[r], tile)
    return tile


def three_parts(x):
    first = x.astype(jnp.bfloat16).astype(jnp.float32)
    second = (x - first).astype(jnp.bfloat16).astype(jnp.float32)
    return first, second, x - first - second


def factor_inverse(diagonal):
    count = BLOCK // TILE
    row_of = lax.broadcasted_iota(jnp.int32, (TILE, BLOCK), 0)
    col_of = lax.broadcasted_iota(jnp.int32, (TILE, BLOCK), 1)
    left = [diagonal[TILE * t:TILE * (t + 1), :] for t in range(count)]
    right = [jnp.where(col_of == row_of + TILE * t, jnp.float32(1.0), jnp.float32(0.0)) for t in range(count)]
    done = []
    for s in range(count):
        own = [spread(left[s][:, TILE * s + c:TILE * s + c + 1]) for c in range(TILE)]
        rest = [[spread(own[c][r:r + 1, :]) for c in range(r + 1)] for r in range(TILE)]
        up = [[spread(side[s][r:r + 1, :]) for r in range(TILE)] for side in (left, right)]
        factor = [[None] * TILE for _ in range(TILE)]
        pivots = {}
        scaled = [None] * TILE
        for c in range(0, TILE, 2):
            a, b, d = rest[c][c], rest[c + 1][c], rest[c + 1][c + 1]
            determinant = a * d - b * b
            over = reciprocal(determinant)
            pivots[c] = (d * over, -(b * over), a * over)
            for r in range(c + 2, TILE):
                factor[r][c] = rest[r][c] * pivots[c][0] + rest[r][c + 1] * pivots[c][1]
                factor[r][c + 1] = rest[r][c] * pivots[c][1] + rest[r][c + 1] * pivots[c][2]
            for r in range(c + 2, TILE):
                for q in range(c + 2, r + 1):
                    rest[r][q] = rest[r][q] - (factor[r][c] * rest[q][c] + factor[r][c + 1] * rest[q][c + 1])
                for rows in up:
                    rows[r] = rows[r] - (factor[r][c] * rows[c] + factor[r][c + 1] * rows[c + 1])
            over_a = reciprocal(a)
            scaled[c] = lax.rsqrt(a) * up[1][c]
            scaled[c + 1] = lax.rsqrt(determinant * over_a) * (up[1][c + 1] - (b * over_a) * up[1][c])
        done.append(rows_of(scaled))
        if s == count - 1:
            break
        down = []
        for rows in up:
            solved = [None] * TILE
            for c in range(TILE - 2, -1, -2):
                p, q, t = pivots[c]
                one = p * rows[c] + q * rows[c + 1]
                two = q * rows[c] + t * rows[c + 1]
                for r in range(TILE - 1, c + 1, -1):
                    one = one - factor[r][c] * solved[r]
                    two = two - factor[r][c + 1] * solved[r]
                solved[c], solved[c + 1] = one, two
            down.append(solved)
        across = [spread(left[s + 1][:, TILE * s + c:TILE * s + c + 1]) for c in range(TILE)]
        for side, solved in zip((left, right), down):
            terms = [across[c] * solved[c] for c in range(TILE)]
            while len(terms) > 1:
                terms = [terms[i] + terms[i + 1] for i in range(0, len(terms), 2)]
            side[s + 1] = side[s + 1] - terms[0]
        if s + 2 < count:
            one, two, three = three_parts(left[s])
            stacked = jnp.concatenate([one, one, two, two, one, three], axis=0).astype(jnp.bfloat16)
            updates = []
            for solved in down:
                one, two, three = three_parts(rows_of(solved))
                updates.append(jnp.concatenate([one, two, one, two, three, one], axis=0).astype(jnp.bfloat16))
            update = lax.dot_general(
                stacked, jnp.concatenate(updates, axis=1), (((0,), (0,)), ((), ())),
                preferred_element_type=jnp.float32,
            )
            for t in range(s + 2, count):
                left[t] = left[t] - update[TILE * t:TILE * (t + 1), :BLOCK]
                right[t] = right[t] - update[TILE * t:TILE * (t + 1), BLOCK:]
    return jnp.concatenate(done, axis=0)


def inverse_kernel(core_ref, own_ref, other_ref, out_ref, rest, sums, lower):
    core = core_ref[0]
    for half_ref, half in ((own_ref, core), (other_ref, 1 - core)):
        for x in range(4):
            for k in range(2):
                for pair in range(4):
                    one = half_ref[8 * pair + x, 16 * k:16 * (k + 1), :]
                    two = half_ref[8 * pair + 4 + x, 16 * k:16 * (k + 1), :]
                    for h in range(2):
                        at = pl.multiple_of(half * 256, 256) + h * 128 + k * 64 + x * 16
                        rest[pl.ds(at, 16), pl.ds(128 * pair, 128)] = jnp.concatenate(
                            [one[:, 64 * h:64 * (h + 1)], two[:, 64 * h:64 * (h + 1)]], axis=1
                        )
    sums[...] = jnp.zeros_like(sums)
    lower[...] = jnp.zeros_like(lower)
    for a in range(0, PANEL, BLOCK):
        b = a + BLOCK
        inverse = factor_inverse(rest[a:b, a:b])
        lower[a:b, a:b] = inverse
        if a > 0:
            lower[a:b, 0:a] = -dot(inverse, sums[a:b, 0:a], 1, 0)
        if b < PANEL:
            upper = dot(inverse, rest[a:b, b:PANEL], 1, 0)
            rest[b:PANEL, b:PANEL] = rest[b:PANEL, b:PANEL] - dot(upper, upper, 0, 0)
            sums[b:PANEL, 0:b] = sums[b:PANEL, 0:b] + dot(upper, lower[a:b, 0:b], 0, 0)
    for k in range(0, PANEL, BLOCK):
        for a in range(0, PANEL, BLOCK):
            turned = jnp.transpose(lower[a:a + BLOCK, k:k + BLOCK]) if a >= k else jnp.zeros((BLOCK, BLOCK), jnp.float32)
            for piece in range(0, BLOCK, 16):
                z, x = divmod((k + piece) // 16, 4)
                to = 128 * x + 16 * z
                out_ref[to:to + 16, a:a + BLOCK] = turned[piece:piece + 16, :]


def inverse_factor(core, own, other):
    shape = (PANEL, PANEL)
    return pl.pallas_call(
        inverse_kernel,
        out_shape=jax.ShapeDtypeStruct(shape, jnp.float32),
        in_specs=[pl.BlockSpec(memory_space=pltpu.SMEM)] + [pl.BlockSpec(memory_space=pltpu.VMEM)] * 2,
        out_specs=pl.BlockSpec(memory_space=pltpu.VMEM),
        scratch_shapes=[pltpu.VMEM(shape, jnp.float32)] * 3,
        compiler_params=pltpu.CompilerParams(vmem_limit_bytes=16 << 20),
        cost_estimate=pl.CostEstimate(flops=4 * PANEL ** 3, bytes_accessed=8 * PANEL ** 2, transcendentals=PANEL),
        name="inverse_factor",
    )(core, own, other)


def prepare_kernel(counts_ref, barrier_ref, border_ref, along_ref, beside_ref, columns, arrived):
    capacity = barrier_ref.shape[1]
    copies = [
        pltpu.make_async_copy(border_ref.at[s, :, pl.ds(0, 128)], columns.at[s], arrived.at[s]) for s in range(2)
    ]
    for copy in copies:
        copy.start()
    position = lax.broadcasted_iota(jnp.int32, (1, capacity), 1)
    for s in range(2):
        weights = jnp.where(position < counts_ref[s], 1.0 / barrier_ref[s:s + 1, :], 0.0)
        copies[s].wait()
        tiles = [jnp.transpose(columns[s, a:a + 128, :])[:TILE, :] for a in range(0, capacity, 128)]
        panel = jnp.concatenate(tiles, axis=1)
        weighted = panel * weights
        for z in range(8):
            along_ref[2 * z + s] = weighted
        for x in range(4):
            beside_ref[2 * x + s] = panel


def prepare(row_counts, barrier, border):
    capacity = border.shape[1]
    vmem = pl.BlockSpec(memory_space=pltpu.VMEM)
    return pl.pallas_call(
        prepare_kernel,
        out_shape=(
            jax.ShapeDtypeStruct((16, TILE, capacity), jnp.float32),
            jax.ShapeDtypeStruct((8, TILE, capacity), jnp.float32),
        ),
        in_specs=[pl.BlockSpec(memory_space=pltpu.SMEM), vmem, pl.BlockSpec(memory_space=pltpu.HBM)],
        out_specs=(vmem, vmem),
        scratch_shapes=[pltpu.VMEM((2, capacity, 128), jnp.float32), pltpu.SemaphoreType.DMA((2,))],
        compiler_params=pltpu.CompilerParams(vmem_limit_bytes=60 << 20),
        name="prepare",
    )(row_counts, barrier, border)


def block_kernel(along_ref, beside_ref, out_ref):
    along = along_ref[...].reshape(16 * TILE, -1)
    beside = beside_ref[...].reshape(8 * TILE, -1)
    part = dot(along, beside, 1, 1)
    quarter = 4 * TILE
    for c in range(2):
        first = part[2 * c * quarter:(2 * c + 1) * quarter]
        second = part[(2 * c + 1) * quarter:(2 * c + 2) * quarter]
        packed = jnp.concatenate([first, second], axis=1)
        for y in range(8):
            out_ref[2 * y + c] = packed


def block_part(along, beside):
    vmem = pl.BlockSpec(memory_space=pltpu.VMEM)
    return pl.pallas_call(
        block_kernel,
        out_shape=jax.ShapeDtypeStruct((16, 4 * TILE, 16 * TILE), jnp.float32),
        in_specs=[vmem, vmem],
        out_specs=vmem,
        compiler_params=pltpu.CompilerParams(vmem_limit_bytes=16 << 20),
        name="block_part",
    )(along, beside)


def product(columns, panel):
    return jnp.einsum(
        "rc,kr->ck", columns, panel,
        precision=lax.Precision.HIGH, preferred_element_type=jnp.float32,
    )


def exchange(array, axes):
    return lax.all_to_all(array, axes, split_axis=0, concat_axis=0, tiled=True)


def body(border, barrier, row_counts):
    capacity = border.shape[1]
    own_cols = border.shape[2]
    n_scen = lax.axis_size("scen")
    rows_owned = own_cols // n_scen
    core = lax.axis_index("core")

    to_along, to_beside = prepare(row_counts, barrier, border)
    along = exchange(to_along, ("z", "core"))
    panel = lax.all_gather(along.reshape(16 * TILE, capacity), "x", axis=0, tiled=True)

    beside = exchange(to_beside, ("x", "core"))
    piece = block_part(along, beside)
    parts = exchange(piece, ("scen", "core"))
    summed = jnp.sum(parts, axis=0)
    copies = jnp.broadcast_to(summed, (32,) + summed.shape)
    own_half = exchange(copies, ("z", "x"))
    other_half = lax.ppermute(own_half, "core", SWAP)
    inverse = inverse_factor(jnp.reshape(core, (1,)), own_half, other_half)

    border, _ = lax.optimization_barrier((border, summed))
    mine = lax.dynamic_index_in_dim(border, core, 0, keepdims=False)
    other = lax.ppermute(lax.dynamic_index_in_dim(border, 1 - core, 0, keepdims=False), "core", SWAP)
    schur_other = product(other, panel)
    schur_mine = product(mine, panel)
    schur_part = schur_mine + lax.ppermute(schur_other, "core", SWAP)
    owned = jnp.sum(exchange(schur_part.reshape(n_scen, rows_owned, PANEL), "scen"), axis=0)
    solved = dot(owned, inverse, 1, 0)
    return solved.reshape(1, 1, rows_owned, PANEL)


def solution(mesh):
    inner = Mesh(mesh.devices.reshape(mesh.shape["scen"], 8, 4, 2), ("scen",) + COL)
    placed = (P("scen", None, COL), P("scen", None), P("scen"))
    return jax.shard_map(
        body, mesh=inner, in_specs=placed, out_specs=P(COL, "scen", None, None), check_vma=False
    )
```

```python
import jax
import jax.numpy as jnp
from jax import lax
from jax.experimental import pallas as pl
from jax.experimental.pallas import tpu as pltpu
from jax.sharding import Mesh, PartitionSpec as P

PANEL = 512
BLOCK = 128
TILE = 8
COL = ("z", "x", "core")
SWAP = [(0, 1), (1, 0)]
AHEAD = [(x, (x + 1) % 4) for x in range(4)]
BEHIND = [(x, (x + 3) % 4) for x in range(4)]


def dot(a, b, dim_a, dim_b):
    return lax.dot_general(
        a, b, (((dim_a,), (dim_b,)), ((), ())),
        precision=lax.Precision.HIGHEST, preferred_element_type=jnp.float32,
    )


def reciprocal(x):
    return pltpu.reciprocal(x, approx=True)


def spread(piece):
    return jnp.broadcast_to(piece, (TILE, BLOCK))


def rows_of(values):
    row_of = lax.broadcasted_iota(jnp.int32, (TILE, BLOCK), 0)
    tile = values[0]
    for r in range(1, TILE):
        tile = jnp.where(row_of == r, values[r], tile)
    return tile


def three_parts(x):
    first = x.astype(jnp.bfloat16).astype(jnp.float32)
    second = (x - first).astype(jnp.bfloat16).astype(jnp.float32)
    return first, second, x - first - second


def factor_inverse(diagonal):
    count = BLOCK // TILE
    row_of = lax.broadcasted_iota(jnp.int32, (TILE, BLOCK), 0)
    col_of = lax.broadcasted_iota(jnp.int32, (TILE, BLOCK), 1)
    left = [diagonal[TILE * t:TILE * (t + 1), :] for t in range(count)]
    right = [jnp.where(col_of == row_of + TILE * t, jnp.float32(1.0), jnp.float32(0.0)) for t in range(count)]
    done = []
    for s in range(count):
        own = [spread(left[s][:, TILE * s + c:TILE * s + c + 1]) for c in range(TILE)]
        rest = [[spread(own[c][r:r + 1, :]) for c in range(r + 1)] for r in range(TILE)]
        up = [[spread(side[s][r:r + 1, :]) for r in range(TILE)] for side in (left, right)]
        factor = [[None] * TILE for _ in range(TILE)]
        pivots = {}
        scaled = [None] * TILE
        for c in range(0, TILE, 2):
            a, b, d = rest[c][c], rest[c + 1][c], rest[c + 1][c + 1]
            determinant = a * d - b * b
            over = reciprocal(determinant)
            pivots[c] = (d * over, -(b * over), a * over)
            for r in range(c + 2, TILE):
                factor[r][c] = rest[r][c] * pivots[c][0] + rest[r][c + 1] * pivots[c][1]
                factor[r][c + 1] = rest[r][c] * pivots[c][1] + rest[r][c + 1] * pivots[c][2]
            for r in range(c + 2, TILE):
                for q in range(c + 2, r + 1):
                    rest[r][q] = rest[r][q] - (factor[r][c] * rest[q][c] + factor[r][c + 1] * rest[q][c + 1])
                for rows in up:
                    rows[r] = rows[r] - (factor[r][c] * rows[c] + factor[r][c + 1] * rows[c + 1])
            over_a = reciprocal(a)
            scaled[c] = lax.rsqrt(a) * up[1][c]
            scaled[c + 1] = lax.rsqrt(determinant * over_a) * (up[1][c + 1] - (b * over_a) * up[1][c])
        done.append(rows_of(scaled))
        if s == count - 1:
            break
        down = []
        for rows in up:
            solved = [None] * TILE
            for c in range(TILE - 2, -1, -2):
                p, q, t = pivots[c]
                one = p * rows[c] + q * rows[c + 1]
                two = q * rows[c] + t * rows[c + 1]
                for r in range(TILE - 1, c + 1, -1):
                    one = one - factor[r][c] * solved[r]
                    two = two - factor[r][c + 1] * solved[r]
                solved[c], solved[c + 1] = one, two
            down.append(solved)
        across = [spread(left[s + 1][:, TILE * s + c:TILE * s + c + 1]) for c in range(TILE)]
        for side, solved in zip((left, right), down):
            terms = [across[c] * solved[c] for c in range(TILE)]
            while len(terms) > 1:
                terms = [terms[i] + terms[i + 1] for i in range(0, len(terms), 2)]
            side[s + 1] = side[s + 1] - terms[0]
        if s + 2 < count:
            one, two, three = three_parts(left[s])
            stacked = jnp.concatenate([one, one, two, two, one, three], axis=0).astype(jnp.bfloat16)
            updates = []
            for solved in down:
                one, two, three = three_parts(rows_of(solved))
                updates.append(jnp.concatenate([one, two, one, two, three, one], axis=0).astype(jnp.bfloat16))
            update = lax.dot_general(
                stacked, jnp.concatenate(updates, axis=1), (((0,), (0,)), ((), ())),
                preferred_element_type=jnp.float32,
            )
            for t in range(s + 2, count):
                left[t] = left[t] - update[TILE * t:TILE * (t + 1), :BLOCK]
                right[t] = right[t] - update[TILE * t:TILE * (t + 1), BLOCK:]
    return jnp.concatenate(done, axis=0)


def inverse_kernel(place_ref, own_ref, other_ref, out_ref, rest, sums, lower):
    core = place_ref[0]
    for half_ref, half in ((own_ref, core), (other_ref, 1 - core)):
        for x in range(4):
            for k in range(2):
                for pair in range(4):
                    one = half_ref[8 * pair + x, 16 * k:16 * (k + 1), :]
                    two = half_ref[8 * pair + 4 + x, 16 * k:16 * (k + 1), :]
                    for h in range(2):
                        at = pl.multiple_of(half * 256, 256) + h * 128 + k * 64 + x * 16
                        rest[pl.ds(at, 16), pl.ds(128 * pair, 128)] = jnp.concatenate(
                            [one[:, 64 * h:64 * (h + 1)], two[:, 64 * h:64 * (h + 1)]], axis=1
                        )
    sums[...] = jnp.zeros_like(sums)
    lower[...] = jnp.zeros_like(lower)
    for a in range(0, PANEL, BLOCK):
        b = a + BLOCK
        inverse = factor_inverse(rest[a:b, a:b])
        lower[a:b, a:b] = inverse
        if a > 0:
            lower[a:b, 0:a] = -dot(inverse, sums[a:b, 0:a], 1, 0)
        if b < PANEL:
            upper = dot(inverse, rest[a:b, b:PANEL], 1, 0)
            rest[b:PANEL, b:PANEL] = rest[b:PANEL, b:PANEL] - dot(upper, upper, 0, 0)
            sums[b:PANEL, 0:b] = sums[b:PANEL, 0:b] + dot(upper, lower[a:b, 0:b], 0, 0)
    slots = []
    for x in range(4):
        ahead = lax.rem(x - place_ref[1] + 4, 4)
        slots.append(jnp.where(ahead == 0, 0, jnp.where(ahead == 3, 1, ahead + 1)))
    for k in range(0, PANEL, BLOCK):
        for a in range(0, PANEL, BLOCK):
            turned = jnp.transpose(lower[a:a + BLOCK, k:k + BLOCK]) if a >= k else jnp.zeros((BLOCK, BLOCK), jnp.float32)
            for piece in range(0, BLOCK, 16):
                z, x = divmod((k + piece) // 16, 4)
                to = pl.multiple_of(slots[x] * 128 + 16 * z, 16)
                out_ref[pl.ds(to, 16), a:a + BLOCK] = turned[piece:piece + 16, :]


def inverse_factor(place, own, other):
    shape = (PANEL, PANEL)
    return pl.pallas_call(
        inverse_kernel,
        out_shape=jax.ShapeDtypeStruct(shape, jnp.float32),
        in_specs=[pl.BlockSpec(memory_space=pltpu.SMEM)] + [pl.BlockSpec(memory_space=pltpu.VMEM)] * 2,
        out_specs=pl.BlockSpec(memory_space=pltpu.VMEM),
        scratch_shapes=[pltpu.VMEM(shape, jnp.float32)] * 3,
        compiler_params=pltpu.CompilerParams(vmem_limit_bytes=16 << 20),
        cost_estimate=pl.CostEstimate(flops=4 * PANEL ** 3, bytes_accessed=8 * PANEL ** 2, transcendentals=PANEL),
        name="inverse_factor",
    )(place, own, other)


def prepare_kernel(counts_ref, barrier_ref, border_ref, along_ref, beside_ref, columns, arrived):
    capacity = barrier_ref.shape[1]
    copies = [
        pltpu.make_async_copy(border_ref.at[s, :, pl.ds(0, 128)], columns.at[s], arrived.at[s]) for s in range(2)
    ]
    for copy in copies:
        copy.start()
    position = lax.broadcasted_iota(jnp.int32, (1, capacity), 1)
    for s in range(2):
        weights = jnp.where(position < counts_ref[s], 1.0 / barrier_ref[s:s + 1, :], 0.0)
        copies[s].wait()
        tiles = [jnp.transpose(columns[s, a:a + 128, :])[:TILE, :] for a in range(0, capacity, 128)]
        panel = jnp.concatenate(tiles, axis=1)
        weighted = panel * weights
        for z in range(8):
            along_ref[2 * z + s] = weighted
        beside_ref[s] = panel


def prepare(row_counts, barrier, border):
    capacity = border.shape[1]
    vmem = pl.BlockSpec(memory_space=pltpu.VMEM)
    return pl.pallas_call(
        prepare_kernel,
        out_shape=(
            jax.ShapeDtypeStruct((16, TILE, capacity), jnp.float32),
            jax.ShapeDtypeStruct((2, TILE, capacity), jnp.float32),
        ),
        in_specs=[pl.BlockSpec(memory_space=pltpu.SMEM), vmem, pl.BlockSpec(memory_space=pltpu.HBM)],
        out_specs=(vmem, vmem),
        scratch_shapes=[pltpu.VMEM((2, capacity, 128), jnp.float32), pltpu.SemaphoreType.DMA((2,))],
        compiler_params=pltpu.CompilerParams(vmem_limit_bytes=60 << 20),
        name="prepare",
    )(row_counts, barrier, border)


def block_kernel(core_ref, along_ref, beside_ref, out_ref):
    along = along_ref[...].reshape(16 * TILE, -1)
    scenario = pl.ds(core_ref[0], 1)
    beside = jnp.concatenate([beside_ref[p, scenario, :, :].reshape(TILE, -1) for p in range(8)], axis=0)
    part = dot(along, beside, 1, 1)
    quarter = 4 * TILE
    for c in range(2):
        first = part[2 * c * quarter:(2 * c + 1) * quarter]
        second = part[(2 * c + 1) * quarter:(2 * c + 2) * quarter]
        packed = jnp.concatenate([first, second], axis=1)
        for y in range(8):
            out_ref[2 * y + c] = packed


def block_part(core, along, beside):
    vmem = pl.BlockSpec(memory_space=pltpu.VMEM)
    return pl.pallas_call(
        block_kernel,
        out_shape=jax.ShapeDtypeStruct((16, 4 * TILE, 16 * TILE), jnp.float32),
        in_specs=[pl.BlockSpec(memory_space=pltpu.SMEM), vmem, vmem],
        out_specs=vmem,
        compiler_params=pltpu.CompilerParams(vmem_limit_bytes=16 << 20),
        name="block_part",
    )(core, along, beside)


def two_parts(x):
    first = x.astype(jnp.bfloat16)
    return first, (x - first.astype(jnp.float32)).astype(jnp.bfloat16)


def product_kernel(columns_ref, *refs):
    *panel_refs, out_ref = refs
    columns, columns_low = two_parts(columns_ref[...])
    panel, panel_low = two_parts(jnp.concatenate([ref[...] for ref in panel_refs], axis=0))
    total = jnp.dot(panel, columns, preferred_element_type=jnp.float32)
    total = total + jnp.dot(panel, columns_low, preferred_element_type=jnp.float32)
    total = total + jnp.dot(panel_low, columns, preferred_element_type=jnp.float32)
    out_ref[...] = jnp.transpose(total)


def product(columns, panels):
    rows, width = columns.shape
    vmem = pl.BlockSpec(memory_space=pltpu.VMEM)
    return pl.pallas_call(
        product_kernel,
        out_shape=jax.ShapeDtypeStruct((width, PANEL), jnp.float32),
        in_specs=[vmem] * (1 + len(panels)),
        out_specs=vmem,
        compiler_params=pltpu.CompilerParams(vmem_limit_bytes=32 << 20),
        cost_estimate=pl.CostEstimate(
            flops=6 * rows * width * PANEL, bytes_accessed=4 * rows * (width + PANEL), transcendentals=0
        ),
        name="product",
    )(columns, *panels)


def exchange(array, axes):
    return lax.all_to_all(array, axes, split_axis=0, concat_axis=0, tiled=True)


def body(border, barrier, row_counts):
    capacity = border.shape[1]
    own_cols = border.shape[2]
    n_scen = lax.axis_size("scen")
    rows_owned = own_cols // n_scen
    core = lax.axis_index("core")
    place = jnp.stack([core, lax.axis_index("x")])

    to_along, to_beside = prepare(row_counts, barrier, border)
    along = exchange(to_along, ("z", "core"))
    beside = lax.all_gather(to_beside, ("x", "core"), axis=0, tiled=False)
    along, beside = lax.optimization_barrier((along, beside))

    shard = along.reshape(16 * TILE, capacity)
    behind = lax.ppermute(shard, "x", AHEAD)
    ahead = lax.ppermute(shard, "x", BEHIND)

    piece = block_part(place, along, beside)
    summed = jnp.sum(exchange(piece, ("scen", "core")), axis=0)
    behind, ahead, summed, later = lax.optimization_barrier((behind, ahead, summed, border))
    copies = jnp.broadcast_to(summed, (32,) + summed.shape)
    own_half = exchange(copies, ("z", "x"))
    other_half = lax.ppermute(own_half, "core", SWAP)
    inverse = inverse_factor(place, own_half, other_half)

    half = 8 * TILE
    panels = (
        shard, behind, ahead, lax.ppermute(behind[:half], "x", AHEAD), lax.ppermute(ahead[half:], "x", BEHIND)
    )
    other = lax.ppermute(lax.dynamic_index_in_dim(later, 1 - core, 0, keepdims=False), "core", SWAP)
    mine = lax.dynamic_index_in_dim(later, core, 0, keepdims=False)
    schur_other = product(other, panels)
    schur_mine = product(mine, panels)
    schur_part = schur_mine + lax.ppermute(schur_other, "core", SWAP)
    owned = jnp.sum(exchange(schur_part.reshape(n_scen, rows_owned, PANEL), "scen"), axis=0)
    solved = dot(owned, inverse, 1, 0)
    return solved.reshape(1, 1, rows_owned, PANEL)


def solution(mesh):
    inner = Mesh(mesh.devices.reshape(mesh.shape["scen"], 8, 4, 2), ("scen",) + COL)
    placed = (P("scen", None, COL), P("scen", None), P("scen"))
    return jax.shard_map(
        body, mesh=inner, in_specs=placed, out_specs=P(COL, "scen", None, None), check_vma=False
    )
```

```python
import jax
import jax.numpy as jnp
from jax import lax
from jax.experimental import pallas as pl
from jax.experimental.pallas import tpu as pltpu
from jax.sharding import Mesh, PartitionSpec as P

PANEL = 512
BLOCK = 128
TILE = 8
COL = ("z", "x", "core")
SWAP = [(0, 1), (1, 0)]
AHEAD = [(x, (x + 1) % 4) for x in range(4)]
BEHIND = [(x, (x + 3) % 4) for x in range(4)]
ONWARD = [(2 * x + c, 2 * ((x + 1 + 2 * c) % 4) + c) for x in range(4) for c in range(2)]


def dot(a, b, dim_a, dim_b):
    return lax.dot_general(
        a, b, (((dim_a,), (dim_b,)), ((), ())),
        precision=lax.Precision.HIGHEST, preferred_element_type=jnp.float32,
    )


def reciprocal(x):
    return pltpu.reciprocal(x, approx=True)


def spread(piece):
    return jnp.broadcast_to(piece, (TILE, BLOCK))


def rows_of(values):
    row_of = lax.broadcasted_iota(jnp.int32, (TILE, BLOCK), 0)
    tile = values[0]
    for r in range(1, TILE):
        tile = jnp.where(row_of == r, values[r], tile)
    return tile


def three_parts(x):
    first = x.astype(jnp.bfloat16).astype(jnp.float32)
    second = (x - first).astype(jnp.bfloat16).astype(jnp.float32)
    return first, second, x - first - second


def factor_inverse(diagonal):
    count = BLOCK // TILE
    row_of = lax.broadcasted_iota(jnp.int32, (TILE, BLOCK), 0)
    col_of = lax.broadcasted_iota(jnp.int32, (TILE, BLOCK), 1)
    left = [diagonal[TILE * t:TILE * (t + 1), :] for t in range(count)]
    right = [jnp.where(col_of == row_of + TILE * t, jnp.float32(1.0), jnp.float32(0.0)) for t in range(count)]
    done = []
    for s in range(count):
        own = [spread(left[s][:, TILE * s + c:TILE * s + c + 1]) for c in range(TILE)]
        rest = [[spread(own[c][r:r + 1, :]) for c in range(r + 1)] for r in range(TILE)]
        up = [[spread(side[s][r:r + 1, :]) for r in range(TILE)] for side in (left, right)]
        factor = [[None] * TILE for _ in range(TILE)]
        pivots = {}
        scaled = [None] * TILE
        for c in range(0, TILE, 2):
            a, b, d = rest[c][c], rest[c + 1][c], rest[c + 1][c + 1]
            determinant = a * d - b * b
            over = reciprocal(determinant)
            pivots[c] = (d * over, -(b * over), a * over)
            for r in range(c + 2, TILE):
                factor[r][c] = rest[r][c] * pivots[c][0] + rest[r][c + 1] * pivots[c][1]
                factor[r][c + 1] = rest[r][c] * pivots[c][1] + rest[r][c + 1] * pivots[c][2]
            for r in range(c + 2, TILE):
                for q in range(c + 2, r + 1):
                    rest[r][q] = rest[r][q] - (factor[r][c] * rest[q][c] + factor[r][c + 1] * rest[q][c + 1])
                for rows in up:
                    rows[r] = rows[r] - (factor[r][c] * rows[c] + factor[r][c + 1] * rows[c + 1])
            over_a = reciprocal(a)
            scaled[c] = lax.rsqrt(a) * up[1][c]
            scaled[c + 1] = lax.rsqrt(determinant * over_a) * (up[1][c + 1] - (b * over_a) * up[1][c])
        done.append(rows_of(scaled))
        if s == count - 1:
            break
        down = []
        for rows in up:
            solved = [None] * TILE
            for c in range(TILE - 2, -1, -2):
                p, q, t = pivots[c]
                one = p * rows[c] + q * rows[c + 1]
                two = q * rows[c] + t * rows[c + 1]
                for r in range(TILE - 1, c + 1, -1):
                    one = one - factor[r][c] * solved[r]
                    two = two - factor[r][c + 1] * solved[r]
                solved[c], solved[c + 1] = one, two
            down.append(solved)
        across = [spread(left[s + 1][:, TILE * s + c:TILE * s + c + 1]) for c in range(TILE)]
        for side, solved in zip((left, right), down):
            terms = [across[c] * solved[c] for c in range(TILE)]
            while len(terms) > 1:
                terms = [terms[i] + terms[i + 1] for i in range(0, len(terms), 2)]
            side[s + 1] = side[s + 1] - terms[0]
        if s + 2 < count:
            one, two, three = three_parts(left[s])
            stacked = jnp.concatenate([one, one, two, two, one, three], axis=0).astype(jnp.bfloat16)
            updates = []
            for solved in down:
                one, two, three = three_parts(rows_of(solved))
                updates.append(jnp.concatenate([one, two, one, two, three, one], axis=0).astype(jnp.bfloat16))
            update = lax.dot_general(
                stacked, jnp.concatenate(updates, axis=1), (((0,), (0,)), ((), ())),
                preferred_element_type=jnp.float32,
            )
            for t in range(s + 2, count):
                left[t] = left[t] - update[TILE * t:TILE * (t + 1), :BLOCK]
                right[t] = right[t] - update[TILE * t:TILE * (t + 1), BLOCK:]
    return jnp.concatenate(done, axis=0)


def inverse_kernel(place_ref, own_ref, other_ref, out_ref, rest, sums, lower):
    core = place_ref[0]
    for half_ref, half in ((own_ref, core), (other_ref, 1 - core)):
        for x in range(4):
            for k in range(2):
                for pair in range(4):
                    one = half_ref[8 * pair + x, 16 * k:16 * (k + 1), :]
                    two = half_ref[8 * pair + 4 + x, 16 * k:16 * (k + 1), :]
                    for h in range(2):
                        at = pl.multiple_of(half * 256, 256) + h * 128 + k * 64 + x * 16
                        rest[pl.ds(at, 16), pl.ds(128 * pair, 128)] = jnp.concatenate(
                            [one[:, 64 * h:64 * (h + 1)], two[:, 64 * h:64 * (h + 1)]], axis=1
                        )
    sums[...] = jnp.zeros_like(sums)
    lower[...] = jnp.zeros_like(lower)
    for a in range(0, PANEL, BLOCK):
        b = a + BLOCK
        inverse = factor_inverse(rest[a:b, a:b])
        lower[a:b, a:b] = inverse
        if a > 0:
            lower[a:b, 0:a] = -dot(inverse, sums[a:b, 0:a], 1, 0)
        if b < PANEL:
            upper = dot(inverse, rest[a:b, b:PANEL], 1, 0)
            rest[b:PANEL, b:PANEL] = rest[b:PANEL, b:PANEL] - dot(upper, upper, 0, 0)
            sums[b:PANEL, 0:b] = sums[b:PANEL, 0:b] + dot(upper, lower[a:b, 0:b], 0, 0)
    slots = []
    for x in range(4):
        ahead = lax.rem(x - place_ref[1] + 4, 4)
        slots.append(jnp.where(ahead == 0, 0, jnp.where(ahead == 3, 1, ahead + 1)))
    for k in range(0, PANEL, BLOCK):
        for a in range(0, PANEL, BLOCK):
            turned = jnp.transpose(lower[a:a + BLOCK, k:k + BLOCK]) if a >= k else jnp.zeros((BLOCK, BLOCK), jnp.float32)
            for piece in range(0, BLOCK, 16):
                z, x = divmod((k + piece) // 16, 4)
                to = pl.multiple_of(slots[x] * 128 + 16 * z, 16)
                out_ref[pl.ds(to, 16), a:a + BLOCK] = turned[piece:piece + 16, :]


def inverse_factor(place, own, other):
    shape = (PANEL, PANEL)
    return pl.pallas_call(
        inverse_kernel,
        out_shape=jax.ShapeDtypeStruct(shape, jnp.float32),
        in_specs=[pl.BlockSpec(memory_space=pltpu.SMEM)] + [pl.BlockSpec(memory_space=pltpu.VMEM)] * 2,
        out_specs=pl.BlockSpec(memory_space=pltpu.VMEM),
        scratch_shapes=[pltpu.VMEM(shape, jnp.float32)] * 3,
        compiler_params=pltpu.CompilerParams(vmem_limit_bytes=16 << 20),
        cost_estimate=pl.CostEstimate(flops=4 * PANEL ** 3, bytes_accessed=8 * PANEL ** 2, transcendentals=PANEL),
        name="inverse_factor",
    )(place, own, other)


def prepare_kernel(place_ref, counts_ref, barrier_ref, border_ref, along_ref, beside_ref, other_ref, columns, arrived, moved):
    capacity = barrier_ref.shape[1]
    copies = [
        pltpu.make_async_copy(border_ref.at[s, :, pl.ds(0, 128)], columns.at[s], arrived.at[s]) for s in range(2)
    ]
    for copy in copies:
        copy.start()
    other = pltpu.make_async_copy(border_ref.at[1 - place_ref[0]], other_ref, moved)
    other.start()
    position = lax.broadcasted_iota(jnp.int32, (1, capacity), 1)
    for s in range(2):
        weights = jnp.where(position < counts_ref[s], 1.0 / barrier_ref[s:s + 1, :], 0.0)
        copies[s].wait()
        tiles = [jnp.transpose(columns[s, a:a + 128, :])[:TILE, :] for a in range(0, capacity, 128)]
        panel = jnp.concatenate(tiles, axis=1)
        weighted = panel * weights
        for z in range(8):
            along_ref[2 * z + s] = weighted
        beside_ref[s] = panel
    other.wait()


def prepare(place, row_counts, barrier, border):
    capacity = border.shape[1]
    vmem = pl.BlockSpec(memory_space=pltpu.VMEM)
    return pl.pallas_call(
        prepare_kernel,
        out_shape=(
            jax.ShapeDtypeStruct((16, TILE, capacity), jnp.float32),
            jax.ShapeDtypeStruct((2, TILE, capacity), jnp.float32),
            jax.ShapeDtypeStruct(border.shape[1:], jnp.float32),
        ),
        in_specs=[pl.BlockSpec(memory_space=pltpu.SMEM)] * 2 + [vmem, pl.BlockSpec(memory_space=pltpu.HBM)],
        out_specs=(vmem, vmem, pl.BlockSpec(memory_space=pltpu.HBM)),
        scratch_shapes=[
            pltpu.VMEM((2, capacity, 128), jnp.float32),
            pltpu.SemaphoreType.DMA((2,)),
            pltpu.SemaphoreType.DMA(()),
        ],
        compiler_params=pltpu.CompilerParams(vmem_limit_bytes=60 << 20),
        name="prepare",
    )(place, row_counts, barrier, border)


def block_kernel(core_ref, along_ref, beside_ref, out_ref):
    along = along_ref[...].reshape(16 * TILE, -1)
    scenario = pl.ds(core_ref[0], 1)
    beside = jnp.concatenate([beside_ref[p, scenario, :, :].reshape(TILE, -1) for p in range(8)], axis=0)
    part = dot(along, beside, 1, 1)
    quarter = 4 * TILE
    for c in range(2):
        first = part[2 * c * quarter:(2 * c + 1) * quarter]
        second = part[(2 * c + 1) * quarter:(2 * c + 2) * quarter]
        packed = jnp.concatenate([first, second], axis=1)
        for y in range(8):
            out_ref[2 * y + c] = packed


def block_part(core, along, beside):
    vmem = pl.BlockSpec(memory_space=pltpu.VMEM)
    return pl.pallas_call(
        block_kernel,
        out_shape=jax.ShapeDtypeStruct((16, 4 * TILE, 16 * TILE), jnp.float32),
        in_specs=[pl.BlockSpec(memory_space=pltpu.SMEM), vmem, vmem],
        out_specs=vmem,
        compiler_params=pltpu.CompilerParams(vmem_limit_bytes=16 << 20),
        name="block_part",
    )(core, along, beside)


def two_parts(x):
    first = x.astype(jnp.bfloat16)
    return first, (x - first.astype(jnp.float32)).astype(jnp.bfloat16)


def product_kernel(columns_ref, *refs):
    *panel_refs, out_ref = refs
    columns, columns_low = two_parts(columns_ref[...])
    panel, panel_low = two_parts(jnp.concatenate([ref[...] for ref in panel_refs], axis=0))
    total = jnp.dot(panel, columns, preferred_element_type=jnp.float32)
    total = total + jnp.dot(panel, columns_low, preferred_element_type=jnp.float32)
    total = total + jnp.dot(panel_low, columns, preferred_element_type=jnp.float32)
    out_ref[...] = jnp.transpose(total)


def product(columns, panels):
    rows, width = columns.shape
    vmem = pl.BlockSpec(memory_space=pltpu.VMEM)
    return pl.pallas_call(
        product_kernel,
        out_shape=jax.ShapeDtypeStruct((width, PANEL), jnp.float32),
        in_specs=[vmem] * (1 + len(panels)),
        out_specs=vmem,
        compiler_params=pltpu.CompilerParams(vmem_limit_bytes=32 << 20),
        cost_estimate=pl.CostEstimate(
            flops=6 * rows * width * PANEL, bytes_accessed=4 * rows * (width + PANEL), transcendentals=0
        ),
        name="product",
    )(columns, *panels)


def exchange(array, axes):
    return lax.all_to_all(array, axes, split_axis=0, concat_axis=0, tiled=True)


def body(border, barrier, row_counts):
    capacity = border.shape[1]
    own_cols = border.shape[2]
    n_scen = lax.axis_size("scen")
    rows_owned = own_cols // n_scen
    core = lax.axis_index("core")
    place = jnp.stack([core, lax.axis_index("x")])

    to_along, to_beside, to_other = prepare(place, row_counts, barrier, border)
    along = exchange(to_along, ("z", "core"))
    beside = lax.all_gather(to_beside, ("x", "core"), axis=0, tiled=False)
    along, beside = lax.optimization_barrier((along, beside))

    shard = along.reshape(16 * TILE, capacity)
    behind = lax.ppermute(shard, "x", AHEAD)
    ahead = lax.ppermute(shard, "x", BEHIND)

    piece = block_part(place, along, beside)
    summed = jnp.sum(exchange(piece, ("scen", "core")), axis=0)
    behind, ahead, summed, to_other = lax.optimization_barrier((behind, ahead, summed, to_other))
    copies = jnp.broadcast_to(summed, (32,) + summed.shape)
    own_half = exchange(copies, ("z", "x"))
    other_half = lax.ppermute(own_half, "core", SWAP)
    inverse = inverse_factor(place, own_half, other_half)

    onward = lax.ppermute(jnp.where(core == 0, behind, ahead), ("x", "core"), ONWARD)
    panels = (shard, behind, ahead, onward)
    other = lax.ppermute(to_other, "core", SWAP)
    mine = lax.dynamic_index_in_dim(border, core, 0, keepdims=False)
    schur_other = product(other, panels)
    schur_mine = product(mine, panels)
    schur_part = schur_mine + lax.ppermute(schur_other, "core", SWAP)
    owned = jnp.sum(exchange(schur_part.reshape(n_scen, rows_owned, PANEL), "scen"), axis=0)
    solved = dot(owned, inverse, 1, 0)
    return solved.reshape(1, 1, rows_owned, PANEL)


def solution(mesh):
    inner = Mesh(mesh.devices.reshape(mesh.shape["scen"], 8, 4, 2), ("scen",) + COL)
    placed = (P("scen", None, COL), P("scen", None), P("scen"))
    return jax.shard_map(
        body, mesh=inner, in_specs=placed, out_specs=P(COL, "scen", None, None), check_vma=False
    )
```

```python
import jax
import jax.numpy as jnp
from jax import lax
from jax.experimental import pallas as pl
from jax.experimental.pallas import tpu as pltpu
from jax.sharding import Mesh, PartitionSpec as P

PANEL = 512
BLOCK = 128
TILE = 8
COL = ("z", "x", "core")
SWAP = [(0, 1), (1, 0)]
AHEAD = [(x, (x + 1) % 4) for x in range(4)]
BEHIND = [(x, (x + 3) % 4) for x in range(4)]
ONWARD = [(2 * x + c, 2 * ((x + 1 + 2 * c) % 4) + c) for x in range(4) for c in range(2)]


def dot(a, b, dim_a, dim_b):
    return lax.dot_general(
        a, b, (((dim_a,), (dim_b,)), ((), ())),
        precision=lax.Precision.HIGHEST, preferred_element_type=jnp.float32,
    )


def reciprocal(x):
    return pltpu.reciprocal(x, approx=True)


def spread(piece):
    return jnp.broadcast_to(piece, (TILE, BLOCK))


def rows_of(values):
    row_of = lax.broadcasted_iota(jnp.int32, (TILE, BLOCK), 0)
    tile = values[0]
    for r in range(1, TILE):
        tile = jnp.where(row_of == r, values[r], tile)
    return tile


def three_parts(x):
    first = x.astype(jnp.bfloat16).astype(jnp.float32)
    second = (x - first).astype(jnp.bfloat16).astype(jnp.float32)
    return first, second, x - first - second


def factor_inverse(diagonal):
    count = BLOCK // TILE
    row_of = lax.broadcasted_iota(jnp.int32, (TILE, BLOCK), 0)
    col_of = lax.broadcasted_iota(jnp.int32, (TILE, BLOCK), 1)
    left = [diagonal[TILE * t:TILE * (t + 1), :] for t in range(count)]
    right = [jnp.where(col_of == row_of + TILE * t, jnp.float32(1.0), jnp.float32(0.0)) for t in range(count)]
    done = []
    for s in range(count):
        own = [spread(left[s][:, TILE * s + c:TILE * s + c + 1]) for c in range(TILE)]
        rest = [[spread(own[c][r:r + 1, :]) for c in range(r + 1)] for r in range(TILE)]
        up = [[spread(side[s][r:r + 1, :]) for r in range(TILE)] for side in (left, right)]
        factor = [[None] * TILE for _ in range(TILE)]
        pivots = {}
        scaled = [None] * TILE
        for c in range(0, TILE, 2):
            a, b, d = rest[c][c], rest[c + 1][c], rest[c + 1][c + 1]
            determinant = a * d - b * b
            over = reciprocal(determinant)
            pivots[c] = (d * over, -(b * over), a * over)
            for r in range(c + 2, TILE):
                factor[r][c] = rest[r][c] * pivots[c][0] + rest[r][c + 1] * pivots[c][1]
                factor[r][c + 1] = rest[r][c] * pivots[c][1] + rest[r][c + 1] * pivots[c][2]
            for r in range(c + 2, TILE):
                for q in range(c + 2, r + 1):
                    rest[r][q] = rest[r][q] - (factor[r][c] * rest[q][c] + factor[r][c + 1] * rest[q][c + 1])
                for rows in up:
                    rows[r] = rows[r] - (factor[r][c] * rows[c] + factor[r][c + 1] * rows[c + 1])
            over_a = reciprocal(a)
            scaled[c] = lax.rsqrt(a) * up[1][c]
            scaled[c + 1] = lax.rsqrt(determinant * over_a) * (up[1][c + 1] - (b * over_a) * up[1][c])
        done.append(rows_of(scaled))
        if s == count - 1:
            break
        down = []
        for rows in up:
            solved = [None] * TILE
            for c in range(TILE - 2, -1, -2):
                p, q, t = pivots[c]
                one = p * rows[c] + q * rows[c + 1]
                two = q * rows[c] + t * rows[c + 1]
                for r in range(TILE - 1, c + 1, -1):
                    one = one - factor[r][c] * solved[r]
                    two = two - factor[r][c + 1] * solved[r]
                solved[c], solved[c + 1] = one, two
            down.append(solved)
        across = [spread(left[s + 1][:, TILE * s + c:TILE * s + c + 1]) for c in range(TILE)]
        for side, solved in zip((left, right), down):
            terms = [across[c] * solved[c] for c in range(TILE)]
            while len(terms) > 1:
                terms = [terms[i] + terms[i + 1] for i in range(0, len(terms), 2)]
            side[s + 1] = side[s + 1] - terms[0]
        if s + 2 < count:
            one, two, three = three_parts(left[s])
            stacked = jnp.concatenate([one, one, two, two, one, three], axis=0).astype(jnp.bfloat16)
            updates = []
            for solved in down:
                one, two, three = three_parts(rows_of(solved))
                updates.append(jnp.concatenate([one, two, one, two, three, one], axis=0).astype(jnp.bfloat16))
            update = lax.dot_general(
                stacked, jnp.concatenate(updates, axis=1), (((0,), (0,)), ((), ())),
                preferred_element_type=jnp.float32,
            )
            for t in range(s + 2, count):
                left[t] = left[t] - update[TILE * t:TILE * (t + 1), :BLOCK]
                right[t] = right[t] - update[TILE * t:TILE * (t + 1), BLOCK:]
    return jnp.concatenate(done, axis=0)


def inverse_kernel(place_ref, own_ref, other_ref, out_ref, rest, sums, lower):
    core = place_ref[0]
    for half_ref, half in ((own_ref, core), (other_ref, 1 - core)):
        for x in range(4):
            for k in range(2):
                for pair in range(4):
                    one = half_ref[8 * pair + x, 16 * k:16 * (k + 1), :]
                    two = half_ref[8 * pair + 4 + x, 16 * k:16 * (k + 1), :]
                    for h in range(2):
                        at = pl.multiple_of(half * 256, 256) + h * 128 + k * 64 + x * 16
                        rest[pl.ds(at, 16), pl.ds(128 * pair, 128)] = jnp.concatenate(
                            [one[:, 64 * h:64 * (h + 1)], two[:, 64 * h:64 * (h + 1)]], axis=1
                        )
    sums[...] = jnp.zeros_like(sums)
    lower[...] = jnp.zeros_like(lower)
    for a in range(0, PANEL, BLOCK):
        b = a + BLOCK
        inverse = factor_inverse(rest[a:b, a:b])
        lower[a:b, a:b] = inverse
        if a > 0:
            lower[a:b, 0:a] = -dot(inverse, sums[a:b, 0:a], 1, 0)
        if b < PANEL:
            upper = dot(inverse, rest[a:b, b:PANEL], 1, 0)
            rest[b:PANEL, b:PANEL] = rest[b:PANEL, b:PANEL] - dot(upper, upper, 0, 0)
            sums[b:PANEL, 0:b] = sums[b:PANEL, 0:b] + dot(upper, lower[a:b, 0:b], 0, 0)
    slots = []
    for x in range(4):
        ahead = lax.rem(x - place_ref[1] + 4, 4)
        slots.append(jnp.where(ahead == 0, 0, jnp.where(ahead == 3, 1, ahead + 1)))
    for k in range(0, PANEL, BLOCK):
        for a in range(0, PANEL, BLOCK):
            turned = jnp.transpose(lower[a:a + BLOCK, k:k + BLOCK]) if a >= k else jnp.zeros((BLOCK, BLOCK), jnp.float32)
            for piece in range(0, BLOCK, 16):
                z, x = divmod((k + piece) // 16, 4)
                to = pl.multiple_of(slots[x] * 128 + 16 * z, 16)
                out_ref[pl.ds(to, 16), a:a + BLOCK] = turned[piece:piece + 16, :]


def inverse_factor(place, own, other):
    shape = (PANEL, PANEL)
    return pl.pallas_call(
        inverse_kernel,
        out_shape=jax.ShapeDtypeStruct(shape, jnp.float32),
        in_specs=[pl.BlockSpec(memory_space=pltpu.SMEM)] + [pl.BlockSpec(memory_space=pltpu.VMEM)] * 2,
        out_specs=pl.BlockSpec(memory_space=pltpu.VMEM),
        scratch_shapes=[pltpu.VMEM(shape, jnp.float32)] * 3,
        compiler_params=pltpu.CompilerParams(vmem_limit_bytes=16 << 20),
        cost_estimate=pl.CostEstimate(flops=4 * PANEL ** 3, bytes_accessed=8 * PANEL ** 2, transcendentals=PANEL),
        name="inverse_factor",
    )(place, own, other)


def prepare_kernel(place_ref, counts_ref, barrier_ref, border_ref, along_ref, beside_ref, other_ref, columns, arrived, moved):
    capacity = barrier_ref.shape[1]
    copies = [
        pltpu.make_async_copy(border_ref.at[s, :, pl.ds(0, 128)], columns.at[s], arrived.at[s]) for s in range(2)
    ]
    for copy in copies:
        copy.start()
    other = pltpu.make_async_copy(border_ref.at[1 - place_ref[0]], other_ref, moved)
    other.start()
    position = lax.broadcasted_iota(jnp.int32, (1, capacity), 1)
    for s in range(2):
        weights = jnp.where(position < counts_ref[s], 1.0 / barrier_ref[s:s + 1, :], 0.0)
        copies[s].wait()
        tiles = [jnp.transpose(columns[s, a:a + 128, :])[:TILE, :] for a in range(0, capacity, 128)]
        panel = jnp.concatenate(tiles, axis=1)
        weighted = panel * weights
        for z in range(8):
            along_ref[2 * z + s] = weighted
        beside_ref[s] = panel
    other.wait()


def prepare(place, row_counts, barrier, border):
    capacity = border.shape[1]
    vmem = pl.BlockSpec(memory_space=pltpu.VMEM)
    return pl.pallas_call(
        prepare_kernel,
        out_shape=(
            jax.ShapeDtypeStruct((16, TILE, capacity), jnp.float32),
            jax.ShapeDtypeStruct((2, TILE, capacity), jnp.float32),
            jax.ShapeDtypeStruct(border.shape[1:], jnp.float32),
        ),
        in_specs=[pl.BlockSpec(memory_space=pltpu.SMEM)] * 2 + [vmem, pl.BlockSpec(memory_space=pltpu.HBM)],
        out_specs=(vmem, vmem, vmem),
        scratch_shapes=[
            pltpu.VMEM((2, capacity, 128), jnp.float32),
            pltpu.SemaphoreType.DMA((2,)),
            pltpu.SemaphoreType.DMA(()),
        ],
        compiler_params=pltpu.CompilerParams(vmem_limit_bytes=60 << 20),
        name="prepare",
    )(place, row_counts, barrier, border)


def block_kernel(core_ref, along_ref, beside_ref, out_ref):
    along = along_ref[...].reshape(16 * TILE, -1)
    scenario = pl.ds(core_ref[0], 1)
    beside = jnp.concatenate([beside_ref[p, scenario, :, :].reshape(TILE, -1) for p in range(8)], axis=0)
    part = dot(along, beside, 1, 1)
    quarter = 4 * TILE
    for c in range(2):
        first = part[2 * c * quarter:(2 * c + 1) * quarter]
        second = part[(2 * c + 1) * quarter:(2 * c + 2) * quarter]
        packed = jnp.concatenate([first, second], axis=1)
        for y in range(8):
            out_ref[2 * y + c] = packed


def block_part(core, along, beside):
    vmem = pl.BlockSpec(memory_space=pltpu.VMEM)
    return pl.pallas_call(
        block_kernel,
        out_shape=jax.ShapeDtypeStruct((16, 4 * TILE, 16 * TILE), jnp.float32),
        in_specs=[pl.BlockSpec(memory_space=pltpu.SMEM), vmem, vmem],
        out_specs=vmem,
        compiler_params=pltpu.CompilerParams(vmem_limit_bytes=16 << 20),
        name="block_part",
    )(core, along, beside)


def two_parts(x):
    first = x.astype(jnp.bfloat16)
    return first, (x - first.astype(jnp.float32)).astype(jnp.bfloat16)


def product_kernel(columns_ref, *refs):
    *panel_refs, out_ref = refs
    columns, columns_low = two_parts(columns_ref[...])
    panel, panel_low = two_parts(jnp.concatenate([ref[...] for ref in panel_refs], axis=0))
    total = jnp.dot(panel, columns, preferred_element_type=jnp.float32)
    total = total + jnp.dot(panel, columns_low, preferred_element_type=jnp.float32)
    total = total + jnp.dot(panel_low, columns, preferred_element_type=jnp.float32)
    out_ref[...] = jnp.transpose(total)


def product(columns, panels):
    rows, width = columns.shape
    vmem = pl.BlockSpec(memory_space=pltpu.VMEM)
    return pl.pallas_call(
        product_kernel,
        out_shape=jax.ShapeDtypeStruct((width, PANEL), jnp.float32),
        in_specs=[vmem] * (1 + len(panels)),
        out_specs=vmem,
        compiler_params=pltpu.CompilerParams(vmem_limit_bytes=32 << 20),
        cost_estimate=pl.CostEstimate(
            flops=6 * rows * width * PANEL, bytes_accessed=4 * rows * (width + PANEL), transcendentals=0
        ),
        name="product",
    )(columns, *panels)


def exchange(array, axes):
    return lax.all_to_all(array, axes, split_axis=0, concat_axis=0, tiled=True)


def body(border, barrier, row_counts):
    capacity = border.shape[1]
    own_cols = border.shape[2]
    n_scen = lax.axis_size("scen")
    rows_owned = own_cols // n_scen
    core = lax.axis_index("core")
    place = jnp.stack([core, lax.axis_index("x")])

    to_along, to_beside, to_other = prepare(place, row_counts, barrier, border)
    along = exchange(to_along, ("z", "core"))
    beside = lax.all_gather(to_beside, ("x", "core"), axis=0, tiled=False)
    along, beside = lax.optimization_barrier((along, beside))

    shard = along.reshape(16 * TILE, capacity)
    behind = lax.ppermute(shard, "x", AHEAD)
    ahead = lax.ppermute(shard, "x", BEHIND)

    piece = block_part(place, along, beside)
    parts = exchange(piece, ("scen", "core"))
    _, passed_on = lax.optimization_barrier((piece, jnp.where(core == 0, behind, ahead)))
    onward = lax.ppermute(passed_on, ("x", "core"), ONWARD)
    parts, _ = lax.optimization_barrier((parts, passed_on))
    summed = jnp.sum(parts, axis=0)
    summed, to_other = lax.optimization_barrier((summed, to_other))
    copies = jnp.broadcast_to(summed, (32,) + summed.shape)
    own_half = exchange(copies, ("z", "x"))
    other_half = lax.ppermute(own_half, "core", SWAP)
    inverse = inverse_factor(place, own_half, other_half)

    panels = (shard, behind, ahead, onward)
    other = lax.ppermute(to_other, "core", SWAP)
    mine = lax.dynamic_index_in_dim(border, core, 0, keepdims=False)
    schur_other = product(other, panels)
    schur_mine = product(mine, panels)
    schur_part = schur_mine + lax.ppermute(schur_other, "core", SWAP)
    owned = jnp.sum(exchange(schur_part.reshape(n_scen, rows_owned, PANEL), "scen"), axis=0)
    solved = dot(owned, inverse, 1, 0)
    return solved.reshape(1, 1, rows_owned, PANEL)


def solution(mesh):
    inner = Mesh(mesh.devices.reshape(mesh.shape["scen"], 8, 4, 2), ("scen",) + COL)
    placed = (P("scen", None, COL), P("scen", None), P("scen"))
    return jax.shard_map(
        body, mesh=inner, in_specs=placed, out_specs=P(COL, "scen", None, None), check_vma=False
    )
```

```python
import functools
import jax
import jax.numpy as jnp
from jax import lax
from jax.experimental import pallas as pl
from jax.experimental.pallas import tpu as pltpu
from jax.sharding import Mesh, PartitionSpec as P

PANEL = 512
BLOCK = 128
TILE = 8
COL = ("z", "x", "core")
SWAP = [(0, 1), (1, 0)]
AHEAD = [(x, (x + 1) % 4) for x in range(4)]
BEHIND = [(x, (x + 3) % 4) for x in range(4)]
ONWARD = [(2 * x + c, 2 * ((x + 1 + 2 * c) % 4) + c) for x in range(4) for c in range(2)]


def dot(a, b, dim_a, dim_b):
    return lax.dot_general(
        a, b, (((dim_a,), (dim_b,)), ((), ())),
        precision=lax.Precision.HIGHEST, preferred_element_type=jnp.float32,
    )


def two_parts(x):
    first = x.astype(jnp.bfloat16)
    return first, (x - first.astype(jnp.float32)).astype(jnp.bfloat16)


def dot_parts(a, b, dim_a, dim_b):
    a, a_low = two_parts(a)
    b, b_low = two_parts(b)
    return lax.dot_general(
        jnp.concatenate([a, a, a_low], axis=dim_a), jnp.concatenate([b, b_low, b], axis=dim_b),
        (((dim_a,), (dim_b,)), ((), ())), preferred_element_type=jnp.float32,
    )


def reciprocal(x):
    return pltpu.reciprocal(x, approx=True)


def spread(piece):
    return jnp.broadcast_to(piece, (TILE, BLOCK))


def rows_of(values):
    row_of = lax.broadcasted_iota(jnp.int32, (TILE, BLOCK), 0)
    tile = values[0]
    for r in range(1, TILE):
        tile = jnp.where(row_of == r, values[r], tile)
    return tile


def three_parts(x):
    first = x.astype(jnp.bfloat16).astype(jnp.float32)
    second = (x - first).astype(jnp.bfloat16).astype(jnp.float32)
    return first, second, x - first - second


def factor_inverse(diagonal, beside=()):
    count = BLOCK // TILE
    row_of = lax.broadcasted_iota(jnp.int32, (TILE, BLOCK), 0)
    col_of = lax.broadcasted_iota(jnp.int32, (TILE, BLOCK), 1)
    left = [diagonal[TILE * t:TILE * (t + 1), :] for t in range(count)]
    right = [jnp.where(col_of == row_of + TILE * t, jnp.float32(1.0), jnp.float32(0.0)) for t in range(count)]
    done = []
    beside = list(beside)
    for s in range(count):
        share = -(-len(beside) // (count - s))
        for step in beside[:share]:
            step()
        beside = beside[share:]
        own = [spread(left[s][:, TILE * s + c:TILE * s + c + 1]) for c in range(TILE)]
        rest = [[spread(own[c][r:r + 1, :]) for c in range(r + 1)] for r in range(TILE)]
        up = [[spread(side[s][r:r + 1, :]) for r in range(TILE)] for side in (left, right)]
        factor = [[None] * TILE for _ in range(TILE)]
        pivots = {}
        scaled = [None] * TILE
        for c in range(0, TILE, 2):
            a, b, d = rest[c][c], rest[c + 1][c], rest[c + 1][c + 1]
            determinant = a * d - b * b
            over = reciprocal(determinant)
            pivots[c] = (d * over, -(b * over), a * over)
            for r in range(c + 2, TILE):
                factor[r][c] = rest[r][c] * pivots[c][0] + rest[r][c + 1] * pivots[c][1]
                factor[r][c + 1] = rest[r][c] * pivots[c][1] + rest[r][c + 1] * pivots[c][2]
            for r in range(c + 2, TILE):
                for q in range(c + 2, r + 1):
                    rest[r][q] = rest[r][q] - (factor[r][c] * rest[q][c] + factor[r][c + 1] * rest[q][c + 1])
                for rows in up:
                    rows[r] = rows[r] - (factor[r][c] * rows[c] + factor[r][c + 1] * rows[c + 1])
            over_a = reciprocal(a)
            scaled[c] = lax.rsqrt(a) * up[1][c]
            scaled[c + 1] = lax.rsqrt(determinant * over_a) * (up[1][c + 1] - (b * over_a) * up[1][c])
        done.append(rows_of(scaled))
        if s == count - 1:
            break
        down = []
        for rows in up:
            solved = [None] * TILE
            for c in range(TILE - 2, -1, -2):
                p, q, t = pivots[c]
                one = p * rows[c] + q * rows[c + 1]
                two = q * rows[c] + t * rows[c + 1]
                for r in range(TILE - 1, c + 1, -1):
                    one = one - factor[r][c] * solved[r]
                    two = two - factor[r][c + 1] * solved[r]
                solved[c], solved[c + 1] = one, two
            down.append(solved)
        across = [spread(left[s + 1][:, TILE * s + c:TILE * s + c + 1]) for c in range(TILE)]
        for side, solved in zip((left, right), down):
            terms = [across[c] * solved[c] for c in range(TILE)]
            while len(terms) > 1:
                terms = [terms[i] + terms[i + 1] for i in range(0, len(terms), 2)]
            side[s + 1] = side[s + 1] - terms[0]
        if s + 2 < count:
            one, two, three = three_parts(left[s])
            stacked = jnp.concatenate([one, one, two, two, one, three], axis=0).astype(jnp.bfloat16)
            updates = []
            for solved in down:
                one, two, three = three_parts(rows_of(solved))
                updates.append(jnp.concatenate([one, two, one, two, three, one], axis=0).astype(jnp.bfloat16))
            update = lax.dot_general(
                stacked, jnp.concatenate(updates, axis=1), (((0,), (0,)), ((), ())),
                preferred_element_type=jnp.float32,
            )
            for t in range(s + 2, count):
                left[t] = left[t] - update[TILE * t:TILE * (t + 1), :BLOCK]
                right[t] = right[t] - update[TILE * t:TILE * (t + 1), BLOCK:]
    return jnp.concatenate(done, axis=0)


def inverse_kernel(place_ref, own_ref, other_ref, out_ref, rest, sums, lower):
    core = place_ref[0]
    for half_ref, half in ((own_ref, core), (other_ref, 1 - core)):
        for x in range(4):
            for k in range(2):
                for pair in range(4):
                    one = half_ref[8 * pair + x, 16 * k:16 * (k + 1), :]
                    two = half_ref[8 * pair + 4 + x, 16 * k:16 * (k + 1), :]
                    for h in range(2):
                        at = pl.multiple_of(half * 256, 256) + h * 128 + k * 64 + x * 16
                        rest[pl.ds(at, 16), pl.ds(128 * pair, 128)] = jnp.concatenate(
                            [one[:, 64 * h:64 * (h + 1)], two[:, 64 * h:64 * (h + 1)]], axis=1
                        )
    slots = []
    for x in range(4):
        ahead = lax.rem(x - place_ref[1] + 4, 4)
        slots.append(jnp.where(ahead == 0, 0, jnp.where(ahead == 3, 1, ahead + 1)))

    def write(row, column, block):
        turned = None if block is None else jnp.transpose(block)
        for piece in range(0, BLOCK, 16):
            z, x = divmod((column + piece) // 16, 4)
            to = pl.multiple_of(slots[x] * 128 + 16 * z, 16)
            values = jnp.zeros((16, BLOCK), jnp.float32) if turned is None else turned[piece:piece + 16, :]
            out_ref[pl.ds(to, 16), row:row + BLOCK] = values

    starts = range(0, PANEL, BLOCK)
    at = {a: slice(a, a + BLOCK) for a in starts}
    beside = [functools.partial(write, a, k, None) for a in starts for k in starts if k > a]
    diagonal = rest[at[0], at[0]]
    for a in starts:
        inverse = factor_inverse(diagonal, beside)
        beside = []
        later = [i for i in starts if i > a]
        upper = {}
        if later:
            near = later[0]
            upper[near] = dot_parts(inverse, rest[at[a], at[near]], 1, 0)
            diagonal = rest[at[near], at[near]] - dot_parts(upper[near], upper[near], 0, 0)

        def finish(k, a=a, inverse=inverse):
            block = inverse if k == a else -dot_parts(inverse, sums[at[a], at[k]], 1, 0)
            lower[at[a], at[k]] = block
            write(a, k, block)

        def above(j, a=a, inverse=inverse, upper=upper):
            upper[j] = dot_parts(inverse, rest[at[a], at[j]], 1, 0)

        def update(i, j, upper=upper):
            rest[at[i], at[j]] = rest[at[i], at[j]] - dot_parts(upper[i], upper[j], 0, 0)

        def gather(i, k, a=a, upper=upper):
            term = dot_parts(upper[i], lower[at[a], at[k]], 0, 0)
            sums[at[i], at[k]] = term if k == a else sums[at[i], at[k]] + term

        beside += [functools.partial(above, j) for j in later[1:]]
        beside += [functools.partial(update, i, j) for i in later for j in later if j >= i and j > later[0]]
        beside += [functools.partial(finish, k) for k in starts if k <= a]
        beside += [functools.partial(gather, i, k) for i in later for k in starts if k <= a]
    for step in beside:
        step()


def inverse_factor(place, own, other):
    shape = (PANEL, PANEL)
    return pl.pallas_call(
        inverse_kernel,
        out_shape=jax.ShapeDtypeStruct(shape, jnp.float32),
        in_specs=[pl.BlockSpec(memory_space=pltpu.SMEM)] + [pl.BlockSpec(memory_space=pltpu.VMEM)] * 2,
        out_specs=pl.BlockSpec(memory_space=pltpu.VMEM),
        scratch_shapes=[pltpu.VMEM(shape, jnp.float32)] * 3,
        compiler_params=pltpu.CompilerParams(vmem_limit_bytes=16 << 20),
        cost_estimate=pl.CostEstimate(flops=4 * PANEL ** 3, bytes_accessed=8 * PANEL ** 2, transcendentals=PANEL),
        name="inverse_factor",
    )(place, own, other)


def prepare_kernel(counts_ref, barrier_ref, border_ref, along_ref, beside_ref, other_ref, columns, arrived, moved):
    capacity = barrier_ref.shape[1]
    copies = [
        pltpu.make_async_copy(border_ref.at[s, :, pl.ds(0, 128)], columns.at[s], arrived.at[s]) for s in range(2)
    ]
    for copy in copies:
        copy.start()
    other = pltpu.make_async_copy(border_ref.at[1 - lax.axis_index("core")], other_ref, moved)
    other.start()
    position = lax.broadcasted_iota(jnp.int32, (1, capacity), 1)
    for s in range(2):
        weights = jnp.where(position < counts_ref[s], 1.0 / barrier_ref[s:s + 1, :], 0.0)
        copies[s].wait()
        tiles = [jnp.transpose(columns[s, a:a + 128, :])[:TILE, :] for a in range(0, capacity, 128)]
        panel = jnp.concatenate(tiles, axis=1)
        weighted = panel * weights
        for z in range(8):
            along_ref[2 * z + s] = weighted
        beside_ref[s] = panel
    other.wait()


def prepare(row_counts, barrier, border):
    capacity = border.shape[1]
    vmem = pl.BlockSpec(memory_space=pltpu.VMEM)
    return pl.pallas_call(
        prepare_kernel,
        out_shape=(
            jax.ShapeDtypeStruct((16, TILE, capacity), jnp.float32),
            jax.ShapeDtypeStruct((2, TILE, capacity), jnp.float32),
            jax.ShapeDtypeStruct(border.shape[1:], jnp.float32),
        ),
        in_specs=[pl.BlockSpec(memory_space=pltpu.SMEM), vmem, pl.BlockSpec(memory_space=pltpu.HBM)],
        out_specs=(vmem, vmem, vmem),
        scratch_shapes=[
            pltpu.VMEM((2, capacity, 128), jnp.float32),
            pltpu.SemaphoreType.DMA((2,)),
            pltpu.SemaphoreType.DMA(()),
        ],
        compiler_params=pltpu.CompilerParams(vmem_limit_bytes=60 << 20),
        name="prepare",
    )(row_counts, barrier, border)


def block_kernel(core_ref, along_ref, beside_ref, out_ref):
    along = along_ref[...].reshape(16 * TILE, -1)
    scenario = pl.ds(core_ref[0], 1)
    beside = jnp.concatenate([beside_ref[p, scenario, :, :].reshape(TILE, -1) for p in range(8)], axis=0)
    part = dot_parts(along, beside, 1, 1)
    quarter = 4 * TILE
    for c in range(2):
        first = part[2 * c * quarter:(2 * c + 1) * quarter]
        second = part[(2 * c + 1) * quarter:(2 * c + 2) * quarter]
        packed = jnp.concatenate([first, second], axis=1)
        for y in range(8):
            out_ref[2 * y + c] = packed


def block_part(core, along, beside):
    vmem = pl.BlockSpec(memory_space=pltpu.VMEM)
    return pl.pallas_call(
        block_kernel,
        out_shape=jax.ShapeDtypeStruct((16, 4 * TILE, 16 * TILE), jnp.float32),
        in_specs=[pl.BlockSpec(memory_space=pltpu.SMEM), vmem, vmem],
        out_specs=vmem,
        compiler_params=pltpu.CompilerParams(vmem_limit_bytes=16 << 20),
        name="block_part",
    )(core, along, beside)


def product_kernel(columns_ref, *refs):
    *panel_refs, out_ref = refs
    panel = jnp.concatenate([ref[...] for ref in panel_refs], axis=0)
    columns, columns_low = two_parts(columns_ref[...])
    panel, panel_low = two_parts(panel)
    total = jnp.dot(panel, columns, preferred_element_type=jnp.float32)
    total = total + jnp.dot(panel, columns_low, preferred_element_type=jnp.float32)
    total = total + jnp.dot(panel_low, columns, preferred_element_type=jnp.float32)
    out_ref[:, out_ref.shape[1] - total.shape[0]:] = jnp.transpose(total)


def further_kernel(columns_ref, panel_ref, before_ref, out_ref):
    out_ref[:, :before_ref.shape[1]] = before_ref[...]
    product_kernel(columns_ref, panel_ref, out_ref)


def product(columns, panels, before=None):
    rows, width = columns.shape
    fresh = sum(panel.shape[0] for panel in panels)
    done = () if before is None else (before,)
    vmem = pl.BlockSpec(memory_space=pltpu.VMEM)
    return pl.pallas_call(
        further_kernel if done else product_kernel,
        out_shape=jax.ShapeDtypeStruct((width, fresh + sum(b.shape[1] for b in done)), jnp.float32),
        in_specs=[vmem] * (1 + len(panels) + len(done)),
        out_specs=vmem,
        compiler_params=pltpu.CompilerParams(vmem_limit_bytes=32 << 20),
        cost_estimate=pl.CostEstimate(
            flops=6 * rows * width * fresh, bytes_accessed=4 * rows * (width + fresh), transcendentals=0
        ),
        name="further" if done else "product",
    )(columns, *panels, *done)


def exchange(array, axes):
    return lax.all_to_all(array, axes, split_axis=0, concat_axis=0, tiled=True)


def body(border, barrier, row_counts):
    capacity = border.shape[1]
    own_cols = border.shape[2]
    n_scen = lax.axis_size("scen")
    rows_owned = own_cols // n_scen
    core = lax.axis_index("core")
    place = jnp.stack([core, lax.axis_index("x")])

    to_along, to_beside, to_other = prepare(row_counts, barrier, border)
    along = exchange(to_along, ("z", "core"))
    beside = lax.all_gather(to_beside, ("x", "core"), axis=0, tiled=False)
    along, beside = lax.optimization_barrier((along, beside))

    shard = along.reshape(16 * TILE, capacity)
    behind = lax.ppermute(shard, "x", AHEAD)
    ahead = lax.ppermute(shard, "x", BEHIND)

    piece = block_part(place, along, beside)
    parts = exchange(piece, ("scen", "core"))
    _, passed_on = lax.optimization_barrier((piece, jnp.where(core == 0, behind, ahead)))
    onward = lax.ppermute(passed_on, ("x", "core"), ONWARD)
    parts, _ = lax.optimization_barrier((parts, passed_on))
    summed = jnp.sum(parts, axis=0)
    summed, to_other = lax.optimization_barrier((summed, to_other))
    copies = jnp.broadcast_to(summed, (32,) + summed.shape)
    own_half = exchange(copies, ("z", "x"))
    other_half = lax.ppermute(own_half, "core", SWAP)
    inverse = inverse_factor(place, own_half, other_half)

    other = lax.ppermute(to_other, "core", SWAP)
    mine = lax.dynamic_index_in_dim(border, core, 0, keepdims=False)
    schur_other = product(other, (shard, behind, ahead))
    schur_mine = product(mine, (shard, behind, ahead))
    onward, schur_other, schur_mine = lax.optimization_barrier((onward, schur_other, schur_mine))
    schur_other = product(other, (onward,), schur_other)
    schur_mine = product(mine, (onward,), schur_mine)
    schur_part = schur_mine + lax.ppermute(schur_other, "core", SWAP)
    owned = jnp.sum(exchange(schur_part.reshape(n_scen, rows_owned, PANEL), "scen"), axis=0)
    solved = dot(owned, inverse, 1, 0)
    return solved.reshape(1, 1, rows_owned, PANEL)


def solution(mesh):
    inner = Mesh(mesh.devices.reshape(mesh.shape["scen"], 8, 4, 2), ("scen",) + COL)
    placed = (P("scen", None, COL), P("scen", None), P("scen"))
    return jax.shard_map(
        body, mesh=inner, in_specs=placed, out_specs=P(COL, "scen", None, None), check_vma=False
    )
```

```python
import functools
import jax
import jax.numpy as jnp
from jax import lax
from jax.experimental import pallas as pl
from jax.experimental.pallas import tpu as pltpu
from jax.sharding import Mesh, PartitionSpec as P

PANEL = 512
BLOCK = 128
TILE = 8
COL = ("z", "x", "core")
SWAP = [(0, 1), (1, 0)]
AHEAD = [(x, (x + 1) % 4) for x in range(4)]
BEHIND = [(x, (x + 3) % 4) for x in range(4)]
ONWARD = [(2 * x + c, 2 * ((x + 1 + 2 * c) % 4) + c) for x in range(4) for c in range(2)]


def dot(a, b, dim_a, dim_b):
    return lax.dot_general(
        a, b, (((dim_a,), (dim_b,)), ((), ())),
        precision=lax.Precision.HIGHEST, preferred_element_type=jnp.float32,
    )


def two_parts(x):
    first = x.astype(jnp.bfloat16)
    return first, (x - first.astype(jnp.float32)).astype(jnp.bfloat16)


def dot_parts(a, b, dim_a, dim_b):
    a, a_low = two_parts(a)
    b, b_low = two_parts(b)
    return lax.dot_general(
        jnp.concatenate([a, a, a_low], axis=dim_a), jnp.concatenate([b, b_low, b], axis=dim_b),
        (((dim_a,), (dim_b,)), ((), ())), preferred_element_type=jnp.float32,
    )


def reciprocal(x):
    return pltpu.reciprocal(x, approx=True)


def spread(piece):
    return jnp.broadcast_to(piece, (TILE, BLOCK))


def rows_of(values):
    row_of = lax.broadcasted_iota(jnp.int32, (TILE, BLOCK), 0)
    tile = values[0]
    for r in range(1, TILE):
        tile = jnp.where(row_of == r, values[r], tile)
    return tile


def three_parts(x):
    first = x.astype(jnp.bfloat16).astype(jnp.float32)
    second = (x - first).astype(jnp.bfloat16).astype(jnp.float32)
    return first, second, x - first - second


def factor_inverse(diagonal, beside=()):
    count = BLOCK // TILE
    row_of = lax.broadcasted_iota(jnp.int32, (TILE, BLOCK), 0)
    col_of = lax.broadcasted_iota(jnp.int32, (TILE, BLOCK), 1)
    left = [diagonal[TILE * t:TILE * (t + 1), :] for t in range(count)]
    right = [jnp.where(col_of == row_of + TILE * t, jnp.float32(1.0), jnp.float32(0.0)) for t in range(count)]
    done = []
    beside = list(beside)
    for s in range(count):
        share = -(-len(beside) // (count - s))
        for step in beside[:share]:
            step()
        beside = beside[share:]
        own = [spread(left[s][:, TILE * s + c:TILE * s + c + 1]) for c in range(TILE)]
        rest = [[spread(own[c][r:r + 1, :]) for c in range(r + 1)] for r in range(TILE)]
        up = [[spread(side[s][r:r + 1, :]) for r in range(TILE)] for side in (left, right)]
        factor = [[None] * TILE for _ in range(TILE)]
        pivots = {}
        scaled = [None] * TILE
        for c in range(0, TILE, 2):
            a, b, d = rest[c][c], rest[c + 1][c], rest[c + 1][c + 1]
            determinant = a * d - b * b
            over = reciprocal(determinant)
            pivots[c] = (d * over, -(b * over), a * over)
            for r in range(c + 2, TILE):
                factor[r][c] = rest[r][c] * pivots[c][0] + rest[r][c + 1] * pivots[c][1]
                factor[r][c + 1] = rest[r][c] * pivots[c][1] + rest[r][c + 1] * pivots[c][2]
            for r in range(c + 2, TILE):
                for q in range(c + 2, r + 1):
                    rest[r][q] = rest[r][q] - (factor[r][c] * rest[q][c] + factor[r][c + 1] * rest[q][c + 1])
                for rows in up:
                    rows[r] = rows[r] - (factor[r][c] * rows[c] + factor[r][c + 1] * rows[c + 1])
            over_a = reciprocal(a)
            scaled[c] = lax.rsqrt(a) * up[1][c]
            scaled[c + 1] = lax.rsqrt(determinant * over_a) * (up[1][c + 1] - (b * over_a) * up[1][c])
        done.append(rows_of(scaled))
        if s == count - 1:
            break
        down = []
        for rows in up:
            solved = [None] * TILE
            for c in range(TILE - 2, -1, -2):
                p, q, t = pivots[c]
                one = p * rows[c] + q * rows[c + 1]
                two = q * rows[c] + t * rows[c + 1]
                for r in range(TILE - 1, c + 1, -1):
                    one = one - factor[r][c] * solved[r]
                    two = two - factor[r][c + 1] * solved[r]
                solved[c], solved[c + 1] = one, two
            down.append(solved)
        across = [spread(left[s + 1][:, TILE * s + c:TILE * s + c + 1]) for c in range(TILE)]
        for side, solved in zip((left, right), down):
            terms = [across[c] * solved[c] for c in range(TILE)]
            while len(terms) > 1:
                terms = [terms[i] + terms[i + 1] for i in range(0, len(terms), 2)]
            side[s + 1] = side[s + 1] - terms[0]
        if s + 2 < count:
            one, two, three = three_parts(left[s])
            stacked = jnp.concatenate([one, one, two, two, one, three], axis=0).astype(jnp.bfloat16)
            updates = []
            for solved in down:
                one, two, three = three_parts(rows_of(solved))
                updates.append(jnp.concatenate([one, two, one, two, three, one], axis=0).astype(jnp.bfloat16))
            update = lax.dot_general(
                stacked, jnp.concatenate(updates, axis=1), (((0,), (0,)), ((), ())),
                preferred_element_type=jnp.float32,
            )
            for t in range(s + 2, count):
                left[t] = left[t] - update[TILE * t:TILE * (t + 1), :BLOCK]
                right[t] = right[t] - update[TILE * t:TILE * (t + 1), BLOCK:]
    return jnp.concatenate(done, axis=0)


def inverse_kernel(place_ref, own_ref, other_ref, out_ref, rest, sums, lower):
    first = place_ref[0] == 0
    side = BLOCK // 2
    for z in range(8):
        for x in range(4):
            own, other = own_ref[4 * z + x], other_ref[4 * z + x]
            halves = [jnp.where(first, own, other), jnp.where(first, other, own)]
            middle = jnp.concatenate([half[16:16 + TILE, :side] for half in halves], axis=0)
            pieces = [halves[0][:16, :side], halves[0][:16, side:], middle, halves[1][:16, :side], halves[1][:16, side:]]
            for d, piece in enumerate(pieces):
                to = 64 * ((z + d) % 8) + 16 * x
                rest[to:to + 16, side * z:side * (z + 1)] = piece
    low = lax.broadcasted_iota(jnp.int32, (BLOCK, BLOCK), 0) >= side
    near = lax.broadcasted_iota(jnp.int32, (BLOCK, BLOCK), 1) < side
    for i in range(0, PANEL, BLOCK):
        for j in range(i, PANEL, BLOCK):
            here, there = rest[j:j + BLOCK, i:i + BLOCK], rest[i:i + BLOCK, j:j + BLOCK]
            turned = jnp.transpose(there)
            if j == i:
                rest[j:j + BLOCK, i:i + BLOCK] = jnp.where(low | near, here, turned)
            elif j == i + 2 * BLOCK:
                rest[j:j + BLOCK, i:i + BLOCK] = jnp.where(low & near, turned, here)
            elif j == i + 3 * BLOCK:
                rest[j:j + BLOCK, i:i + BLOCK] = turned
    slots = []
    for x in range(4):
        ahead = lax.rem(x - place_ref[1] + 4, 4)
        slots.append(jnp.where(ahead == 0, 0, jnp.where(ahead == 3, 1, ahead + 1)))

    def write(row, column, block):
        turned = None if block is None else jnp.transpose(block)
        for piece in range(0, BLOCK, 16):
            z, x = divmod((column + piece) // 16, 4)
            to = pl.multiple_of(slots[x] * 128 + 16 * z, 16)
            values = jnp.zeros((16, BLOCK), jnp.float32) if turned is None else turned[piece:piece + 16, :]
            out_ref[pl.ds(to, 16), row:row + BLOCK] = values

    starts = range(0, PANEL, BLOCK)
    at = {a: slice(a, a + BLOCK) for a in starts}
    beside = [functools.partial(write, a, k, None) for a in starts for k in starts if k > a]
    diagonal = rest[at[0], at[0]]
    for a in starts:
        inverse = factor_inverse(diagonal, beside)
        beside = []
        later = [i for i in starts if i > a]
        upper = {}
        if later:
            near = later[0]
            upper[near] = dot_parts(inverse, rest[at[near], at[a]], 1, 1)
            diagonal = rest[at[near], at[near]] - dot_parts(upper[near], upper[near], 0, 0)

        def finish(k, a=a, inverse=inverse):
            block = inverse if k == a else -dot_parts(inverse, sums[at[a], at[k]], 1, 0)
            lower[at[a], at[k]] = block
            write(a, k, block)

        def above(j, a=a, inverse=inverse, upper=upper):
            upper[j] = dot_parts(inverse, rest[at[j], at[a]], 1, 1)

        def update(i, j, upper=upper):
            rest[at[j], at[i]] = rest[at[j], at[i]] - dot_parts(upper[j], upper[i], 0, 0)

        def gather(i, k, a=a, upper=upper):
            term = dot_parts(upper[i], lower[at[a], at[k]], 0, 0)
            sums[at[i], at[k]] = term if k == a else sums[at[i], at[k]] + term

        beside += [functools.partial(above, j) for j in later[1:]]
        beside += [functools.partial(update, i, j) for i in later for j in later if j >= i and j > later[0]]
        beside += [functools.partial(finish, k) for k in starts if k <= a]
        beside += [functools.partial(gather, i, k) for i in later for k in starts if k <= a]
    for step in beside:
        step()


def inverse_factor(place, own, other):
    shape = (PANEL, PANEL)
    return pl.pallas_call(
        inverse_kernel,
        out_shape=jax.ShapeDtypeStruct(shape, jnp.float32),
        in_specs=[pl.BlockSpec(memory_space=pltpu.SMEM)] + [pl.BlockSpec(memory_space=pltpu.VMEM)] * 2,
        out_specs=pl.BlockSpec(memory_space=pltpu.VMEM),
        scratch_shapes=[pltpu.VMEM(shape, jnp.float32)] * 3,
        compiler_params=pltpu.CompilerParams(vmem_limit_bytes=16 << 20),
        cost_estimate=pl.CostEstimate(flops=4 * PANEL ** 3, bytes_accessed=8 * PANEL ** 2, transcendentals=PANEL),
        name="inverse_factor",
    )(place, own, other)


def prepare_kernel(counts_ref, barrier_ref, border_ref, along_ref, beside_ref, other_ref, columns, arrived, moved):
    capacity = barrier_ref.shape[1]
    copies = [
        pltpu.make_async_copy(border_ref.at[s, :, pl.ds(0, 128)], columns.at[s], arrived.at[s]) for s in range(2)
    ]
    for copy in copies:
        copy.start()
    other = pltpu.make_async_copy(border_ref.at[1 - lax.axis_index("core")], other_ref, moved)
    other.start()
    position = lax.broadcasted_iota(jnp.int32, (1, capacity), 1)
    for s in range(2):
        weights = jnp.where(position < counts_ref[s], 1.0 / barrier_ref[s:s + 1, :], 0.0)
        copies[s].wait()
        tiles = [jnp.transpose(columns[s, a:a + 128, :])[:TILE, :] for a in range(0, capacity, 128)]
        panel = jnp.concatenate(tiles, axis=1)
        weighted = panel * weights
        for z in range(8):
            along_ref[2 * z + s] = weighted
        beside_ref[s] = panel
    other.wait()


def prepare(row_counts, barrier, border):
    capacity = border.shape[1]
    vmem = pl.BlockSpec(memory_space=pltpu.VMEM)
    return pl.pallas_call(
        prepare_kernel,
        out_shape=(
            jax.ShapeDtypeStruct((16, TILE, capacity), jnp.float32),
            jax.ShapeDtypeStruct((2, TILE, capacity), jnp.float32),
            jax.ShapeDtypeStruct(border.shape[1:], jnp.float32),
        ),
        in_specs=[pl.BlockSpec(memory_space=pltpu.SMEM), vmem, pl.BlockSpec(memory_space=pltpu.HBM)],
        out_specs=(vmem, vmem, vmem),
        scratch_shapes=[
            pltpu.VMEM((2, capacity, 128), jnp.float32),
            pltpu.SemaphoreType.DMA((2,)),
            pltpu.SemaphoreType.DMA(()),
        ],
        compiler_params=pltpu.CompilerParams(vmem_limit_bytes=60 << 20),
        name="prepare",
    )(row_counts, barrier, border)


def block_kernel(along_ref, beside_ref, out_ref, part_ref):
    along = along_ref[...].reshape(16 * TILE, -1)
    scenario = pl.ds(lax.axis_index("core"), 1)
    beside = jnp.concatenate([beside_ref[p, scenario, :, :].reshape(TILE, -1) for p in range(8)], axis=0)
    part_ref[...] = dot_parts(along, beside, 1, 1)
    z = lax.axis_index("z")
    rows = [part_ref[pl.ds(pl.multiple_of(lax.rem(z + d, 8) * 16, 16), 16), :] for d in range(5)]
    packed = [
        jnp.concatenate(
            [
                jnp.concatenate([rows[3 * c], rows[3 * c + 1]], axis=1),
                jnp.concatenate([rows[2][TILE * c:TILE * (c + 1)]] * 2, axis=1),
            ],
            axis=0,
        )
        for c in range(2)
    ]
    for y in range(8):
        for c in range(2):
            out_ref[2 * y + c] = packed[c]


def block_part(along, beside):
    vmem = pl.BlockSpec(memory_space=pltpu.VMEM)
    return pl.pallas_call(
        block_kernel,
        out_shape=jax.ShapeDtypeStruct((16, 3 * TILE, 16 * TILE), jnp.float32),
        in_specs=[vmem, vmem],
        out_specs=vmem,
        scratch_shapes=[pltpu.VMEM((16 * TILE, 8 * TILE), jnp.float32)],
        compiler_params=pltpu.CompilerParams(vmem_limit_bytes=16 << 20),
        name="block_part",
    )(along, beside)


def product_kernel(columns_ref, *refs):
    *panel_refs, out_ref = refs
    panel = jnp.concatenate([ref[...] for ref in panel_refs], axis=0)
    columns, columns_low = two_parts(columns_ref[...])
    panel, panel_low = two_parts(panel)
    total = jnp.dot(panel, columns, preferred_element_type=jnp.float32)
    total = total + jnp.dot(panel, columns_low, preferred_element_type=jnp.float32)
    total = total + jnp.dot(panel_low, columns, preferred_element_type=jnp.float32)
    out_ref[:, out_ref.shape[1] - total.shape[0]:] = jnp.transpose(total)


def further_kernel(columns_ref, panel_ref, before_ref, out_ref):
    out_ref[:, :before_ref.shape[1]] = before_ref[...]
    product_kernel(columns_ref, panel_ref, out_ref)


def product(columns, panels, before=None):
    rows, width = columns.shape
    fresh = sum(panel.shape[0] for panel in panels)
    done = () if before is None else (before,)
    vmem = pl.BlockSpec(memory_space=pltpu.VMEM)
    return pl.pallas_call(
        further_kernel if done else product_kernel,
        out_shape=jax.ShapeDtypeStruct((width, fresh + sum(b.shape[1] for b in done)), jnp.float32),
        in_specs=[vmem] * (1 + len(panels) + len(done)),
        out_specs=vmem,
        compiler_params=pltpu.CompilerParams(vmem_limit_bytes=32 << 20),
        cost_estimate=pl.CostEstimate(
            flops=6 * rows * width * fresh, bytes_accessed=4 * rows * (width + fresh), transcendentals=0
        ),
        name="further" if done else "product",
    )(columns, *panels, *done)


def exchange(array, axes):
    return lax.all_to_all(array, axes, split_axis=0, concat_axis=0, tiled=True)


def body(border, barrier, row_counts):
    capacity = border.shape[1]
    own_cols = border.shape[2]
    n_scen = lax.axis_size("scen")
    rows_owned = own_cols // n_scen
    core = lax.axis_index("core")
    place = jnp.stack([core, lax.axis_index("x")])

    to_along, to_beside, to_other = prepare(row_counts, barrier, border)
    along = exchange(to_along, ("z", "core"))
    beside = lax.all_gather(to_beside, ("x", "core"), axis=0, tiled=False)
    along, beside = lax.optimization_barrier((along, beside))

    shard = along.reshape(16 * TILE, capacity)
    behind = lax.ppermute(shard, "x", AHEAD)
    ahead = lax.ppermute(shard, "x", BEHIND)

    piece = block_part(along, beside)
    parts = exchange(piece, ("scen", "core"))
    _, passed_on = lax.optimization_barrier((piece, jnp.where(core == 0, behind, ahead)))
    onward = lax.ppermute(passed_on, ("x", "core"), ONWARD)
    parts, _ = lax.optimization_barrier((parts, passed_on))
    summed = jnp.sum(parts, axis=0)
    summed, to_other = lax.optimization_barrier((summed, to_other))
    copies = jnp.broadcast_to(summed, (32,) + summed.shape)
    own_half = exchange(copies, ("z", "x"))
    other_half = lax.ppermute(own_half, "core", SWAP)
    inverse = inverse_factor(place, own_half, other_half)

    other = lax.ppermute(to_other, "core", SWAP)
    mine = lax.dynamic_index_in_dim(border, core, 0, keepdims=False)
    schur_other = product(other, (shard, behind, ahead))
    schur_mine = product(mine, (shard, behind, ahead))
    onward, schur_other, schur_mine = lax.optimization_barrier((onward, schur_other, schur_mine))
    schur_other = product(other, (onward,), schur_other)
    schur_mine = product(mine, (onward,), schur_mine)
    schur_part = schur_mine + lax.ppermute(schur_other, "core", SWAP)
    owned = jnp.sum(exchange(schur_part.reshape(n_scen, rows_owned, PANEL), "scen"), axis=0)
    solved = dot(owned, inverse, 1, 0)
    return solved.reshape(1, 1, rows_owned, PANEL)


def solution(mesh):
    inner = Mesh(mesh.devices.reshape(mesh.shape["scen"], 8, 4, 2), ("scen",) + COL)
    placed = (P("scen", None, COL), P("scen", None), P("scen"))
    return jax.shard_map(
        body, mesh=inner, in_specs=placed, out_specs=P(COL, "scen", None, None), check_vma=False
    )
```

```python
import functools
import jax
import jax.numpy as jnp
from jax import lax
from jax.experimental import pallas as pl
from jax.experimental.pallas import tpu as pltpu
from jax.sharding import Mesh, PartitionSpec as P

PANEL = 512
BLOCK = 128
TILE = 8
COL = ("z", "x", "core")
SWAP = [(0, 1), (1, 0)]
AHEAD = [(x, (x + 1) % 4) for x in range(4)]
BEHIND = [(x, (x + 3) % 4) for x in range(4)]
ONWARD = [(2 * x + c, 2 * ((x + 1 + 2 * c) % 4) + c) for x in range(4) for c in range(2)]


def dot(a, b, dim_a, dim_b):
    return lax.dot_general(
        a, b, (((dim_a,), (dim_b,)), ((), ())),
        precision=lax.Precision.HIGHEST, preferred_element_type=jnp.float32,
    )


def two_parts(x):
    first = x.astype(jnp.bfloat16)
    return first, (x - first.astype(jnp.float32)).astype(jnp.bfloat16)


def dot_parts(a, b, dim_a, dim_b):
    a, a_low = two_parts(a)
    b, b_low = two_parts(b)
    return lax.dot_general(
        jnp.concatenate([a, a, a_low], axis=dim_a), jnp.concatenate([b, b_low, b], axis=dim_b),
        (((dim_a,), (dim_b,)), ((), ())), preferred_element_type=jnp.float32,
    )


def reciprocal(x):
    return pltpu.reciprocal(x, approx=True)


def spread(piece):
    return jnp.broadcast_to(piece, (TILE, BLOCK))


def rows_of(values):
    row_of = lax.broadcasted_iota(jnp.int32, (TILE, BLOCK), 0)
    tile = values[0]
    for r in range(1, TILE):
        tile = jnp.where(row_of == r, values[r], tile)
    return tile


def three_parts(x):
    first = x.astype(jnp.bfloat16).astype(jnp.float32)
    second = (x - first).astype(jnp.bfloat16).astype(jnp.float32)
    return first, second, x - first - second


def factor_inverse(diagonal, beside=()):
    count = BLOCK // TILE
    row_of = lax.broadcasted_iota(jnp.int32, (TILE, BLOCK), 0)
    col_of = lax.broadcasted_iota(jnp.int32, (TILE, BLOCK), 1)
    left = [diagonal[TILE * t:TILE * (t + 1), :] for t in range(count)]
    right = [jnp.where(col_of == row_of + TILE * t, jnp.float32(1.0), jnp.float32(0.0)) for t in range(count)]
    done = []
    beside = list(beside)
    for s in range(count):
        share = -(-len(beside) // (count - s))
        for step in beside[:share]:
            step()
        beside = beside[share:]
        own = [spread(left[s][:, TILE * s + c:TILE * s + c + 1]) for c in range(TILE)]
        rest = [[spread(own[c][r:r + 1, :]) for c in range(r + 1)] for r in range(TILE)]
        up = [[spread(side[s][r:r + 1, :]) for r in range(TILE)] for side in (left, right)]
        factor = [[None] * TILE for _ in range(TILE)]
        pivots = {}
        scaled = [None] * TILE
        for c in range(0, TILE, 2):
            a, b, d = rest[c][c], rest[c + 1][c], rest[c + 1][c + 1]
            determinant = a * d - b * b
            over = reciprocal(determinant)
            pivots[c] = (d * over, -(b * over), a * over)
            for r in range(c + 2, TILE):
                factor[r][c] = rest[r][c] * pivots[c][0] + rest[r][c + 1] * pivots[c][1]
                factor[r][c + 1] = rest[r][c] * pivots[c][1] + rest[r][c + 1] * pivots[c][2]
            for r in range(c + 2, TILE):
                for q in range(c + 2, r + 1):
                    rest[r][q] = rest[r][q] - (factor[r][c] * rest[q][c] + factor[r][c + 1] * rest[q][c + 1])
                for rows in up:
                    rows[r] = rows[r] - (factor[r][c] * rows[c] + factor[r][c + 1] * rows[c + 1])
            over_a = reciprocal(a)
            scaled[c] = lax.rsqrt(a) * up[1][c]
            scaled[c + 1] = lax.rsqrt(determinant * over_a) * (up[1][c + 1] - (b * over_a) * up[1][c])
        done.append(rows_of(scaled))
        if s == count - 1:
            break
        down = []
        for rows in up:
            solved = [None] * TILE
            for c in range(TILE - 2, -1, -2):
                p, q, t = pivots[c]
                one = p * rows[c] + q * rows[c + 1]
                two = q * rows[c] + t * rows[c + 1]
                for r in range(TILE - 1, c + 1, -1):
                    one = one - factor[r][c] * solved[r]
                    two = two - factor[r][c + 1] * solved[r]
                solved[c], solved[c + 1] = one, two
            down.append(solved)
        across = [spread(left[s + 1][:, TILE * s + c:TILE * s + c + 1]) for c in range(TILE)]
        for side, solved in zip((left, right), down):
            terms = [across[c] * solved[c] for c in range(TILE)]
            while len(terms) > 1:
                terms = [terms[i] + terms[i + 1] for i in range(0, len(terms), 2)]
            side[s + 1] = side[s + 1] - terms[0]
        if s + 2 < count:
            one, two, three = three_parts(left[s])
            stacked = jnp.concatenate([one, one, two, two, one, three], axis=0).astype(jnp.bfloat16)
            updates = []
            for solved in down:
                one, two, three = three_parts(rows_of(solved))
                updates.append(jnp.concatenate([one, two, one, two, three, one], axis=0).astype(jnp.bfloat16))
            update = lax.dot_general(
                stacked, jnp.concatenate(updates, axis=1), (((0,), (0,)), ((), ())),
                preferred_element_type=jnp.float32,
            )
            for t in range(s + 2, count):
                left[t] = left[t] - update[TILE * t:TILE * (t + 1), :BLOCK]
                right[t] = right[t] - update[TILE * t:TILE * (t + 1), BLOCK:]
    return jnp.concatenate(done, axis=0)


def inverse_kernel(place_ref, own_ref, other_ref, out_ref, rest, sums, lower):
    first = place_ref[0] == 0
    side = BLOCK // 2
    for z in range(8):
        for x in range(4):
            own, other = own_ref[4 * z + x], other_ref[4 * z + x]
            halves = [jnp.where(first, own, other), jnp.where(first, other, own)]
            middle = jnp.concatenate([half[16:16 + TILE, :side] for half in halves], axis=0)
            pieces = [halves[0][:16, :side], halves[0][:16, side:], middle, halves[1][:16, :side], halves[1][:16, side:]]
            for d, piece in enumerate(pieces):
                to = 64 * ((z + d) % 8) + 16 * x
                rest[to:to + 16, side * z:side * (z + 1)] = piece
    low = lax.broadcasted_iota(jnp.int32, (BLOCK, BLOCK), 0) >= side
    near = lax.broadcasted_iota(jnp.int32, (BLOCK, BLOCK), 1) < side
    for i in range(0, PANEL, BLOCK):
        for j in range(i, PANEL, BLOCK):
            here, there = rest[j:j + BLOCK, i:i + BLOCK], rest[i:i + BLOCK, j:j + BLOCK]
            turned = jnp.transpose(there)
            if j == i:
                rest[j:j + BLOCK, i:i + BLOCK] = jnp.where(low | near, here, turned)
            elif j == i + 2 * BLOCK:
                rest[j:j + BLOCK, i:i + BLOCK] = jnp.where(low & near, turned, here)
            elif j == i + 3 * BLOCK:
                rest[j:j + BLOCK, i:i + BLOCK] = turned
    slots = []
    for x in range(4):
        ahead = lax.rem(x - place_ref[1] + 4, 4)
        slots.append(jnp.where(ahead == 0, 0, jnp.where(ahead == 3, 1, ahead + 1)))

    def write(row, column, block):
        turned = None if block is None else jnp.transpose(block)
        for piece in range(0, BLOCK, 16):
            z, x = divmod((column + piece) // 16, 4)
            to = pl.multiple_of(slots[x] * 128 + 16 * z, 16)
            values = jnp.zeros((16, BLOCK), jnp.float32) if turned is None else turned[piece:piece + 16, :]
            out_ref[pl.ds(to, 16), row:row + BLOCK] = values

    starts = range(0, PANEL, BLOCK)
    at = {a: slice(a, a + BLOCK) for a in starts}
    beside = [functools.partial(write, a, k, None) for a in starts for k in starts if k > a]
    diagonal = rest[at[0], at[0]]
    for a in starts:
        inverse = factor_inverse(diagonal, beside)
        beside = []
        later = [i for i in starts if i > a]
        upper = {}
        if later:
            near = later[0]
            upper[near] = dot_parts(inverse, rest[at[near], at[a]], 1, 1)
            diagonal = rest[at[near], at[near]] - dot_parts(upper[near], upper[near], 0, 0)

        def finish(k, a=a, inverse=inverse):
            block = inverse if k == a else -dot_parts(inverse, sums[at[a], at[k]], 1, 0)
            lower[at[a], at[k]] = block
            write(a, k, block)

        def above(j, a=a, inverse=inverse, upper=upper):
            upper[j] = dot_parts(inverse, rest[at[j], at[a]], 1, 1)

        def update(i, j, upper=upper):
            rest[at[j], at[i]] = rest[at[j], at[i]] - dot_parts(upper[j], upper[i], 0, 0)

        def gather(i, k, a=a, upper=upper):
            term = dot_parts(upper[i], lower[at[a], at[k]], 0, 0)
            sums[at[i], at[k]] = term if k == a else sums[at[i], at[k]] + term

        beside += [functools.partial(above, j) for j in later[1:]]
        beside += [functools.partial(update, i, j) for i in later for j in later if j >= i and j > later[0]]
        beside += [functools.partial(finish, k) for k in starts if k <= a]
        beside += [functools.partial(gather, i, k) for i in later for k in starts if k <= a]
    for step in beside:
        step()


def inverse_factor(place, own, other):
    shape = (PANEL, PANEL)
    return pl.pallas_call(
        inverse_kernel,
        out_shape=jax.ShapeDtypeStruct(shape, jnp.float32),
        in_specs=[pl.BlockSpec(memory_space=pltpu.SMEM)] + [pl.BlockSpec(memory_space=pltpu.VMEM)] * 2,
        out_specs=pl.BlockSpec(memory_space=pltpu.VMEM),
        scratch_shapes=[pltpu.VMEM(shape, jnp.float32)] * 3,
        compiler_params=pltpu.CompilerParams(vmem_limit_bytes=16 << 20),
        cost_estimate=pl.CostEstimate(flops=4 * PANEL ** 3, bytes_accessed=8 * PANEL ** 2, transcendentals=PANEL),
        name="inverse_factor",
    )(place, own, other)


def prepare_kernel(counts_ref, barrier_ref, border_ref, along_ref, beside_ref, other_ref, columns, arrived, moved):
    capacity = barrier_ref.shape[1]
    copies = [
        pltpu.make_async_copy(border_ref.at[s, :, pl.ds(0, 128)], columns.at[s], arrived.at[s]) for s in range(2)
    ]
    for copy in copies:
        copy.start()
    other = pltpu.make_async_copy(border_ref.at[1 - lax.axis_index("core")], other_ref, moved)
    other.start()
    position = lax.broadcasted_iota(jnp.int32, (1, capacity), 1)
    for s in range(2):
        weights = jnp.where(position < counts_ref[s], 1.0 / barrier_ref[s:s + 1, :], 0.0)
        copies[s].wait()
        tiles = [jnp.transpose(columns[s, a:a + 128, :])[:TILE, :] for a in range(0, capacity, 128)]
        panel = jnp.concatenate(tiles, axis=1)
        weighted = panel * weights
        for z in range(8):
            along_ref[2 * z + s] = weighted
        beside_ref[s] = panel
    other.wait()


def prepare(row_counts, barrier, border):
    capacity = border.shape[1]
    vmem = pl.BlockSpec(memory_space=pltpu.VMEM)
    return pl.pallas_call(
        prepare_kernel,
        out_shape=(
            jax.ShapeDtypeStruct((16, TILE, capacity), jnp.float32),
            jax.ShapeDtypeStruct((2, TILE, capacity), jnp.float32),
            jax.ShapeDtypeStruct(border.shape[1:], jnp.float32),
        ),
        in_specs=[pl.BlockSpec(memory_space=pltpu.SMEM), vmem, pl.BlockSpec(memory_space=pltpu.HBM)],
        out_specs=(vmem, vmem, vmem),
        scratch_shapes=[
            pltpu.VMEM((2, capacity, 128), jnp.float32),
            pltpu.SemaphoreType.DMA((2,)),
            pltpu.SemaphoreType.DMA(()),
        ],
        compiler_params=pltpu.CompilerParams(vmem_limit_bytes=60 << 20),
        name="prepare",
    )(row_counts, barrier, border)


def block_kernel(along_ref, beside_ref, out_ref, part_ref):
    along = along_ref[...].reshape(16 * TILE, -1)
    scenario = pl.ds(lax.axis_index("core"), 1)
    beside = jnp.concatenate([beside_ref[p, scenario, :, :].reshape(TILE, -1) for p in range(8)], axis=0)
    part_ref[...] = dot_parts(along, beside, 1, 1)
    z = lax.axis_index("z")
    rows = [part_ref[pl.ds(pl.multiple_of(lax.rem(z + d, 8) * 16, 16), 16), :] for d in range(5)]
    packed = [
        jnp.concatenate(
            [
                jnp.concatenate([rows[3 * c], rows[3 * c + 1]], axis=1),
                jnp.concatenate([rows[2][TILE * c:TILE * (c + 1)]] * 2, axis=1),
            ],
            axis=0,
        )
        for c in range(2)
    ]
    for y in range(8):
        for c in range(2):
            out_ref[2 * y + c] = packed[c]


def block_part(along, beside):
    vmem = pl.BlockSpec(memory_space=pltpu.VMEM)
    return pl.pallas_call(
        block_kernel,
        out_shape=jax.ShapeDtypeStruct((16, 3 * TILE, 16 * TILE), jnp.float32),
        in_specs=[vmem, vmem],
        out_specs=vmem,
        scratch_shapes=[pltpu.VMEM((16 * TILE, 8 * TILE), jnp.float32)],
        compiler_params=pltpu.CompilerParams(vmem_limit_bytes=16 << 20),
        name="block_part",
    )(along, beside)


def product_kernel(columns_ref, *refs):
    *panel_refs, out_ref = refs
    panel = jnp.concatenate([ref[...] for ref in panel_refs], axis=0)
    columns, columns_low = two_parts(columns_ref[...])
    panel, panel_low = two_parts(panel)
    total = jnp.dot(panel, columns, preferred_element_type=jnp.float32)
    total = total + jnp.dot(panel, columns_low, preferred_element_type=jnp.float32)
    total = total + jnp.dot(panel_low, columns, preferred_element_type=jnp.float32)
    out_ref[:, out_ref.shape[1] - total.shape[0]:] = jnp.transpose(total)


def further_kernel(columns_ref, panel_ref, before_ref, out_ref):
    out_ref[:, :before_ref.shape[1]] = before_ref[...]
    product_kernel(columns_ref, panel_ref, out_ref)


def product(columns, panels, before=None):
    rows, width = columns.shape
    fresh = sum(panel.shape[0] for panel in panels)
    done = () if before is None else (before,)
    vmem = pl.BlockSpec(memory_space=pltpu.VMEM)
    return pl.pallas_call(
        further_kernel if done else product_kernel,
        out_shape=jax.ShapeDtypeStruct((width, fresh + sum(b.shape[1] for b in done)), jnp.float32),
        in_specs=[vmem] * (1 + len(panels) + len(done)),
        out_specs=vmem,
        compiler_params=pltpu.CompilerParams(vmem_limit_bytes=32 << 20),
        cost_estimate=pl.CostEstimate(
            flops=6 * rows * width * fresh, bytes_accessed=4 * rows * (width + fresh), transcendentals=0
        ),
        name="further" if done else "product",
    )(columns, *panels, *done)


def exchange(array, axes):
    return lax.all_to_all(array, axes, split_axis=0, concat_axis=0, tiled=True)


def body(border, barrier, row_counts):
    capacity = border.shape[1]
    own_cols = border.shape[2]
    n_scen = lax.axis_size("scen")
    rows_owned = own_cols // n_scen
    core = lax.axis_index("core")
    place = jnp.stack([core, lax.axis_index("x")])

    to_along, to_beside, to_other = prepare(row_counts, barrier, border)
    along = exchange(to_along, ("z", "core"))
    beside = lax.all_gather(to_beside, ("x", "core"), axis=0, tiled=False)
    beside, to_other = lax.optimization_barrier((beside, to_other))
    other = lax.ppermute(to_other, "core", SWAP)
    along, beside = lax.optimization_barrier((along, beside))

    shard = along.reshape(16 * TILE, capacity)
    behind = lax.ppermute(shard, "x", AHEAD)
    ahead = lax.ppermute(shard, "x", BEHIND)

    piece = block_part(along, beside)
    parts = exchange(piece, ("scen", "core"))
    _, passed_on = lax.optimization_barrier((piece, jnp.where(core == 0, behind, ahead)))
    onward = lax.ppermute(passed_on, ("x", "core"), ONWARD)
    parts, _ = lax.optimization_barrier((parts, passed_on))
    summed = jnp.sum(parts, axis=0)
    copies = jnp.broadcast_to(summed, (32,) + summed.shape)
    own_half = exchange(copies, ("z", "x"))
    other_half = lax.ppermute(own_half, "core", SWAP)
    inverse = inverse_factor(place, own_half, other_half)

    mine = lax.dynamic_index_in_dim(border, core, 0, keepdims=False)
    schur_other = product(other, (shard, behind, ahead))
    schur_mine = product(mine, (shard, behind, ahead))
    onward, schur_other, schur_mine = lax.optimization_barrier((onward, schur_other, schur_mine))
    schur_other = product(other, (onward,), schur_other)
    schur_mine = product(mine, (onward,), schur_mine)
    schur_part = schur_mine + lax.ppermute(schur_other, "core", SWAP)
    owned = jnp.sum(exchange(schur_part.reshape(n_scen, rows_owned, PANEL), "scen"), axis=0)
    solved = dot(owned, inverse, 1, 0)
    return solved.reshape(1, 1, rows_owned, PANEL)


def solution(mesh):
    inner = Mesh(mesh.devices.reshape(mesh.shape["scen"], 8, 4, 2), ("scen",) + COL)
    placed = (P("scen", None, COL), P("scen", None), P("scen"))
    return jax.shard_map(
        body, mesh=inner, in_specs=placed, out_specs=P(COL, "scen", None, None), check_vma=False
    )
```

```python
import functools
import jax
import jax.numpy as jnp
from jax import lax
from jax.experimental import pallas as pl
from jax.experimental.pallas import tpu as pltpu
from jax.sharding import Mesh, PartitionSpec as P

PANEL = 512
BLOCK = 128
TILE = 8
COL = ("z", "x", "core")
SWAP = [(0, 1), (1, 0)]
AHEAD = [(x, (x + 1) % 4) for x in range(4)]
BEHIND = [(x, (x + 3) % 4) for x in range(4)]
ONWARD = [(2 * x + c, 2 * ((x + 1 + 2 * c) % 4) + c) for x in range(4) for c in range(2)]


def dot(a, b, dim_a, dim_b):
    return lax.dot_general(
        a, b, (((dim_a,), (dim_b,)), ((), ())),
        precision=lax.Precision.HIGHEST, preferred_element_type=jnp.float32,
    )


def two_parts(x):
    first = x.astype(jnp.bfloat16)
    return first, (x - first.astype(jnp.float32)).astype(jnp.bfloat16)


def dot_parts(a, b, dim_a, dim_b):
    a, a_low = two_parts(a)
    b, b_low = two_parts(b)
    return lax.dot_general(
        jnp.concatenate([a, a, a_low], axis=dim_a), jnp.concatenate([b, b_low, b], axis=dim_b),
        (((dim_a,), (dim_b,)), ((), ())), preferred_element_type=jnp.float32,
    )


def reciprocal(x):
    return pltpu.reciprocal(x, approx=True)


def spread(piece):
    return jnp.broadcast_to(piece, (TILE, BLOCK))


def rows_of(values):
    row_of = lax.broadcasted_iota(jnp.int32, (TILE, BLOCK), 0)
    tile = values[0]
    for r in range(1, TILE):
        tile = jnp.where(row_of == r, values[r], tile)
    return tile


def three_parts(x):
    first = x.astype(jnp.bfloat16).astype(jnp.float32)
    second = (x - first).astype(jnp.bfloat16).astype(jnp.float32)
    return first, second, x - first - second


def factor_inverse(diagonal, beside=()):
    count = BLOCK // TILE
    row_of = lax.broadcasted_iota(jnp.int32, (TILE, BLOCK), 0)
    col_of = lax.broadcasted_iota(jnp.int32, (TILE, BLOCK), 1)
    left = [diagonal[TILE * t:TILE * (t + 1), :] for t in range(count)]
    right = [jnp.where(col_of == row_of + TILE * t, jnp.float32(1.0), jnp.float32(0.0)) for t in range(count)]
    done = []
    beside = list(beside)
    for s in range(count):
        share = -(-len(beside) // (count - s))
        for step in beside[:share]:
            step()
        beside = beside[share:]
        own = [spread(left[s][:, TILE * s + c:TILE * s + c + 1]) for c in range(TILE)]
        rest = [[spread(own[c][r:r + 1, :]) for c in range(r + 1)] for r in range(TILE)]
        up = [[spread(side[s][r:r + 1, :]) for r in range(TILE)] for side in (left, right)]
        factor = [[None] * TILE for _ in range(TILE)]
        pivots = {}
        scaled = [None] * TILE
        for c in range(0, TILE, 2):
            a, b, d = rest[c][c], rest[c + 1][c], rest[c + 1][c + 1]
            determinant = a * d - b * b
            over = reciprocal(determinant)
            pivots[c] = (d * over, -(b * over), a * over)
            for r in range(c + 2, TILE):
                factor[r][c] = rest[r][c] * pivots[c][0] + rest[r][c + 1] * pivots[c][1]
                factor[r][c + 1] = rest[r][c] * pivots[c][1] + rest[r][c + 1] * pivots[c][2]
            for r in range(c + 2, TILE):
                for q in range(c + 2, r + 1):
                    rest[r][q] = rest[r][q] - (factor[r][c] * rest[q][c] + factor[r][c + 1] * rest[q][c + 1])
                for rows in up:
                    rows[r] = rows[r] - (factor[r][c] * rows[c] + factor[r][c + 1] * rows[c + 1])
            over_a = reciprocal(a)
            scaled[c] = lax.rsqrt(a) * up[1][c]
            scaled[c + 1] = lax.rsqrt(determinant * over_a) * (up[1][c + 1] - (b * over_a) * up[1][c])
        done.append(rows_of(scaled))
        if s == count - 1:
            break
        down = []
        for rows in up:
            solved = [None] * TILE
            for c in range(TILE - 2, -1, -2):
                p, q, t = pivots[c]
                one = p * rows[c] + q * rows[c + 1]
                two = q * rows[c] + t * rows[c + 1]
                for r in range(TILE - 1, c + 1, -1):
                    one = one - factor[r][c] * solved[r]
                    two = two - factor[r][c + 1] * solved[r]
                solved[c], solved[c + 1] = one, two
            down.append(solved)
        across = [spread(left[s + 1][:, TILE * s + c:TILE * s + c + 1]) for c in range(TILE)]
        for side, solved in zip((left, right), down):
            terms = [across[c] * solved[c] for c in range(TILE)]
            while len(terms) > 1:
                terms = [terms[i] + terms[i + 1] for i in range(0, len(terms), 2)]
            side[s + 1] = side[s + 1] - terms[0]
        if s + 2 < count:
            one, two, three = three_parts(left[s])
            stacked = jnp.concatenate([one, one, two, two, one, three], axis=0).astype(jnp.bfloat16)
            updates = []
            for solved in down:
                one, two, three = three_parts(rows_of(solved))
                updates.append(jnp.concatenate([one, two, one, two, three, one], axis=0).astype(jnp.bfloat16))
            update = lax.dot_general(
                stacked, jnp.concatenate(updates, axis=1), (((0,), (0,)), ((), ())),
                preferred_element_type=jnp.float32,
            )
            for t in range(s + 2, count):
                left[t] = left[t] - update[TILE * t:TILE * (t + 1), :BLOCK]
                right[t] = right[t] - update[TILE * t:TILE * (t + 1), BLOCK:]
    return jnp.concatenate(done, axis=0)


def inverse_kernel(place_ref, own_ref, other_ref, out_ref, rest, sums, lower):
    first = place_ref[0] == 0
    side = BLOCK // 2
    for z in range(8):
        for x in range(4):
            own, other = own_ref[4 * z + x], other_ref[4 * z + x]
            halves = [jnp.where(first, own, other), jnp.where(first, other, own)]
            middle = jnp.concatenate([half[16:16 + TILE, :side] for half in halves], axis=0)
            pieces = [halves[0][:16, :side], halves[0][:16, side:], middle, halves[1][:16, :side], halves[1][:16, side:]]
            for d, piece in enumerate(pieces):
                to = 64 * ((z + d) % 8) + 16 * x
                rest[to:to + 16, side * z:side * (z + 1)] = piece
    low = lax.broadcasted_iota(jnp.int32, (BLOCK, BLOCK), 0) >= side
    near = lax.broadcasted_iota(jnp.int32, (BLOCK, BLOCK), 1) < side
    for i in range(0, PANEL, BLOCK):
        for j in range(i, PANEL, BLOCK):
            here, there = rest[j:j + BLOCK, i:i + BLOCK], rest[i:i + BLOCK, j:j + BLOCK]
            turned = jnp.transpose(there)
            if j == i:
                rest[j:j + BLOCK, i:i + BLOCK] = jnp.where(low | near, here, turned)
            elif j == i + 2 * BLOCK:
                rest[j:j + BLOCK, i:i + BLOCK] = jnp.where(low & near, turned, here)
            elif j == i + 3 * BLOCK:
                rest[j:j + BLOCK, i:i + BLOCK] = turned
    slots = []
    for x in range(4):
        ahead = lax.rem(x - place_ref[1] + 4, 4)
        slots.append(jnp.where(ahead == 0, 0, jnp.where(ahead == 3, 1, ahead + 1)))

    def write(row, column, block):
        turned = None if block is None else jnp.transpose(block)
        for piece in range(0, BLOCK, 16):
            z, x = divmod((column + piece) // 16, 4)
            to = pl.multiple_of(slots[x] * 128 + 16 * z, 16)
            values = jnp.zeros((16, BLOCK), jnp.float32) if turned is None else turned[piece:piece + 16, :]
            out_ref[pl.ds(to, 16), row:row + BLOCK] = values

    starts = range(0, PANEL, BLOCK)
    at = {a: slice(a, a + BLOCK) for a in starts}
    beside = [functools.partial(write, a, k, None) for a in starts for k in starts if k > a]
    diagonal = rest[at[0], at[0]]
    for a in starts:
        inverse = factor_inverse(diagonal, beside)
        beside = []
        later = [i for i in starts if i > a]
        upper = {}
        if later:
            near = later[0]
            upper[near] = dot_parts(inverse, rest[at[near], at[a]], 1, 1)
            diagonal = rest[at[near], at[near]] - dot_parts(upper[near], upper[near], 0, 0)

        def finish(k, a=a, inverse=inverse):
            block = inverse if k == a else -dot_parts(inverse, sums[at[a], at[k]], 1, 0)
            lower[at[a], at[k]] = block
            write(a, k, block)

        def above(j, a=a, inverse=inverse, upper=upper):
            upper[j] = dot_parts(inverse, rest[at[j], at[a]], 1, 1)

        def update(i, j, upper=upper):
            rest[at[j], at[i]] = rest[at[j], at[i]] - dot_parts(upper[j], upper[i], 0, 0)

        def gather(i, k, a=a, upper=upper):
            term = dot_parts(upper[i], lower[at[a], at[k]], 0, 0)
            sums[at[i], at[k]] = term if k == a else sums[at[i], at[k]] + term

        beside += [functools.partial(above, j) for j in later[1:]]
        beside += [functools.partial(update, i, j) for i in later for j in later if j >= i and j > later[0]]
        beside += [functools.partial(finish, k) for k in starts if k <= a]
        beside += [functools.partial(gather, i, k) for i in later for k in starts if k <= a]
    for step in beside:
        step()


def inverse_factor(place, own, other):
    shape = (PANEL, PANEL)
    return pl.pallas_call(
        inverse_kernel,
        out_shape=jax.ShapeDtypeStruct(shape, jnp.float32),
        in_specs=[pl.BlockSpec(memory_space=pltpu.SMEM)] + [pl.BlockSpec(memory_space=pltpu.VMEM)] * 2,
        out_specs=pl.BlockSpec(memory_space=pltpu.VMEM),
        scratch_shapes=[pltpu.VMEM(shape, jnp.float32)] * 3,
        compiler_params=pltpu.CompilerParams(vmem_limit_bytes=16 << 20),
        cost_estimate=pl.CostEstimate(flops=4 * PANEL ** 3, bytes_accessed=8 * PANEL ** 2, transcendentals=PANEL),
        name="inverse_factor",
    )(place, own, other)


def prepare_kernel(counts_ref, barrier_ref, border_ref, along_ref, beside_ref, other_ref, columns, arrived, moved):
    capacity = barrier_ref.shape[1]
    copies = [
        pltpu.make_async_copy(border_ref.at[s, :, pl.ds(0, 128)], columns.at[s], arrived.at[s]) for s in range(2)
    ]
    for copy in copies:
        copy.start()
    other = pltpu.make_async_copy(border_ref.at[1 - lax.axis_index("core")], other_ref, moved)
    other.start()
    position = lax.broadcasted_iota(jnp.int32, (1, capacity), 1)
    for s in range(2):
        weights = jnp.where(position < counts_ref[s], 1.0 / barrier_ref[s:s + 1, :], 0.0)
        copies[s].wait()
        tiles = [jnp.transpose(columns[s, a:a + 128, :])[:TILE, :] for a in range(0, capacity, 128)]
        panel = jnp.concatenate(tiles, axis=1)
        weighted = panel * weights
        for z in range(8):
            along_ref[2 * z + s] = weighted
        beside_ref[s] = panel
    other.wait()


def prepare(row_counts, barrier, border):
    capacity = border.shape[1]
    vmem = pl.BlockSpec(memory_space=pltpu.VMEM)
    return pl.pallas_call(
        prepare_kernel,
        out_shape=(
            jax.ShapeDtypeStruct((16, TILE, capacity), jnp.float32),
            jax.ShapeDtypeStruct((2, TILE, capacity), jnp.float32),
            jax.ShapeDtypeStruct(border.shape[1:], jnp.float32),
        ),
        in_specs=[pl.BlockSpec(memory_space=pltpu.SMEM), vmem, pl.BlockSpec(memory_space=pltpu.HBM)],
        out_specs=(vmem, vmem, vmem),
        scratch_shapes=[
            pltpu.VMEM((2, capacity, 128), jnp.float32),
            pltpu.SemaphoreType.DMA((2,)),
            pltpu.SemaphoreType.DMA(()),
        ],
        compiler_params=pltpu.CompilerParams(vmem_limit_bytes=60 << 20),
        name="prepare",
    )(row_counts, barrier, border)


def block_kernel(along_ref, beside_ref, out_ref, part_ref):
    along = along_ref[...].reshape(16 * TILE, -1)
    scenario = pl.ds(lax.axis_index("core"), 1)
    beside = jnp.concatenate([beside_ref[p, scenario, :, :].reshape(TILE, -1) for p in range(8)], axis=0)
    part_ref[...] = dot_parts(along, beside, 1, 1)
    z = lax.axis_index("z")
    rows = [part_ref[pl.ds(pl.multiple_of(lax.rem(z + d, 8) * 16, 16), 16), :] for d in range(5)]
    packed = [
        jnp.concatenate(
            [
                jnp.concatenate([rows[3 * c], rows[3 * c + 1]], axis=1),
                jnp.concatenate([rows[2][TILE * c:TILE * (c + 1)]] * 2, axis=1),
            ],
            axis=0,
        )
        for c in range(2)
    ]
    for y in range(8):
        for c in range(2):
            out_ref[2 * y + c] = packed[c]


def block_part(along, beside):
    vmem = pl.BlockSpec(memory_space=pltpu.VMEM)
    return pl.pallas_call(
        block_kernel,
        out_shape=jax.ShapeDtypeStruct((16, 3 * TILE, 16 * TILE), jnp.float32),
        in_specs=[vmem, vmem],
        out_specs=vmem,
        scratch_shapes=[pltpu.VMEM((16 * TILE, 8 * TILE), jnp.float32)],
        compiler_params=pltpu.CompilerParams(vmem_limit_bytes=16 << 20),
        name="block_part",
    )(along, beside)


def product_kernel(columns_ref, *refs):
    *panel_refs, out_ref = refs
    panel = jnp.concatenate([ref[...] for ref in panel_refs], axis=0)
    columns, columns_low = two_parts(columns_ref[...])
    panel, panel_low = two_parts(panel)
    total = jnp.dot(panel, columns, preferred_element_type=jnp.float32)
    total = total + jnp.dot(panel, columns_low, preferred_element_type=jnp.float32)
    total = total + jnp.dot(panel_low, columns, preferred_element_type=jnp.float32)
    out_ref[:, out_ref.shape[1] - total.shape[0]:] = jnp.transpose(total)


def further_kernel(columns_ref, panel_ref, before_ref, out_ref):
    out_ref[:, :before_ref.shape[1]] = before_ref[...]
    product_kernel(columns_ref, panel_ref, out_ref)


def product(columns, panels, before=None):
    rows, width = columns.shape
    fresh = sum(panel.shape[0] for panel in panels)
    done = () if before is None else (before,)
    vmem = pl.BlockSpec(memory_space=pltpu.VMEM)
    return pl.pallas_call(
        further_kernel if done else product_kernel,
        out_shape=jax.ShapeDtypeStruct((width, fresh + sum(b.shape[1] for b in done)), jnp.float32),
        in_specs=[vmem] * (1 + len(panels) + len(done)),
        out_specs=vmem,
        compiler_params=pltpu.CompilerParams(vmem_limit_bytes=32 << 20),
        cost_estimate=pl.CostEstimate(
            flops=6 * rows * width * fresh, bytes_accessed=4 * rows * (width + fresh), transcendentals=0
        ),
        name="further" if done else "product",
    )(columns, *panels, *done)


def exchange(array, axes):
    return lax.all_to_all(array, axes, split_axis=0, concat_axis=0, tiled=True)


def body(border, barrier, row_counts):
    capacity = border.shape[1]
    own_cols = border.shape[2]
    n_scen = lax.axis_size("scen")
    rows_owned = own_cols // n_scen
    core = lax.axis_index("core")
    place = jnp.stack([core, lax.axis_index("x")])

    to_along, to_beside, to_other = prepare(row_counts, barrier, border)
    along = exchange(to_along, ("z", "core"))
    beside = lax.all_gather(to_beside, ("x", "core"), axis=0, tiled=False)
    beside, to_other = lax.optimization_barrier((beside, to_other))
    other = lax.ppermute(to_other, "core", SWAP)
    along, beside = lax.optimization_barrier((along, beside))

    shard = along.reshape(16 * TILE, capacity)
    behind = lax.ppermute(shard, "x", AHEAD)
    ahead = lax.ppermute(shard, "x", BEHIND)

    piece = block_part(along, beside)
    parts = exchange(piece, ("scen", "core"))
    _, passed_on = lax.optimization_barrier((piece, jnp.where(core == 0, behind, ahead)))
    onward = lax.ppermute(passed_on, ("x", "core"), ONWARD)
    parts, _ = lax.optimization_barrier((parts, passed_on))
    summed = jnp.sum(parts, axis=0)
    copies = jnp.broadcast_to(summed, (32,) + summed.shape)
    own_half = exchange(copies, ("z", "x"))
    other_half = lax.ppermute(own_half, "core", SWAP)
    inverse = inverse_factor(place, own_half, other_half)

    mine = lax.dynamic_index_in_dim(border, core, 0, keepdims=False)
    schur_other = product(other, (shard, behind, ahead))
    schur_mine = product(mine, (shard, behind, ahead))
    onward, schur_other, schur_mine = lax.optimization_barrier((onward, schur_other, schur_mine))
    schur_other = product(other, (onward,), schur_other)
    schur_mine = product(mine, (onward,), schur_mine)
    schur_part = schur_mine + lax.ppermute(schur_other, "core", SWAP)
    owned = jnp.sum(exchange(schur_part.reshape(n_scen, rows_owned, PANEL), "scen"), axis=0)
    solved = jnp.dot(owned, inverse, precision=lax.Precision.HIGH, preferred_element_type=jnp.float32)
    return solved.reshape(1, 1, rows_owned, PANEL)


def solution(mesh):
    inner = Mesh(mesh.devices.reshape(mesh.shape["scen"], 8, 4, 2), ("scen",) + COL)
    placed = (P("scen", None, COL), P("scen", None), P("scen"))
    return jax.shard_map(
        body, mesh=inner, in_specs=placed, out_specs=P(COL, "scen", None, None), check_vma=False
    )
```

```python
import functools
import jax
import jax.numpy as jnp
from jax import lax
from jax.experimental import pallas as pl
from jax.experimental.pallas import tpu as pltpu
from jax.sharding import Mesh, PartitionSpec as P

PANEL = 512
BLOCK = 128
TILE = 8
COL = ("z", "x", "core")
SWAP = [(0, 1), (1, 0)]
AHEAD = [(x, (x + 1) % 4) for x in range(4)]
BEHIND = [(x, (x + 3) % 4) for x in range(4)]
ONWARD = [(2 * x + c, 2 * ((x + 1 + 2 * c) % 4) + c) for x in range(4) for c in range(2)]


def dot(a, b, dim_a, dim_b):
    return lax.dot_general(
        a, b, (((dim_a,), (dim_b,)), ((), ())),
        precision=lax.Precision.HIGHEST, preferred_element_type=jnp.float32,
    )


def two_parts(x):
    first = x.astype(jnp.bfloat16)
    return first, (x - first.astype(jnp.float32)).astype(jnp.bfloat16)


def dot_parts(a, b, dim_a, dim_b):
    a, a_low = two_parts(a)
    b, b_low = two_parts(b)
    return lax.dot_general(
        jnp.concatenate([a, a, a_low], axis=dim_a), jnp.concatenate([b, b_low, b], axis=dim_b),
        (((dim_a,), (dim_b,)), ((), ())), preferred_element_type=jnp.float32,
    )


def reciprocal(x):
    return pltpu.reciprocal(x, approx=True)


def spread(piece):
    return jnp.broadcast_to(piece, (TILE, BLOCK))


def rows_of(values):
    row_of = lax.broadcasted_iota(jnp.int32, (TILE, BLOCK), 0)
    tile = values[0]
    for r in range(1, TILE):
        tile = jnp.where(row_of == r, values[r], tile)
    return tile


def three_parts(x):
    first = x.astype(jnp.bfloat16).astype(jnp.float32)
    second = (x - first).astype(jnp.bfloat16).astype(jnp.float32)
    return first, second, x - first - second


def factor_inverse(diagonal, beside=()):
    count = BLOCK // TILE
    row_of = lax.broadcasted_iota(jnp.int32, (TILE, BLOCK), 0)
    col_of = lax.broadcasted_iota(jnp.int32, (TILE, BLOCK), 1)
    left = [diagonal[TILE * t:TILE * (t + 1), :] for t in range(count)]
    right = [jnp.where(col_of == row_of + TILE * t, jnp.float32(1.0), jnp.float32(0.0)) for t in range(count)]
    done = []
    beside = list(beside)
    for s in range(count):
        share = -(-len(beside) // (count - s))
        for step in beside[:share]:
            step()
        beside = beside[share:]
        own = [spread(left[s][:, TILE * s + c:TILE * s + c + 1]) for c in range(TILE)]
        rest = [[spread(own[c][r:r + 1, :]) for c in range(r + 1)] for r in range(TILE)]
        up = [[spread(side[s][r:r + 1, :]) for r in range(TILE)] for side in (left, right)]
        factor = [[None] * TILE for _ in range(TILE)]
        pivots = {}
        scaled = [None] * TILE
        for c in range(0, TILE, 2):
            a, b, d = rest[c][c], rest[c + 1][c], rest[c + 1][c + 1]
            determinant = a * d - b * b
            over = reciprocal(determinant)
            pivots[c] = (d * over, -(b * over), a * over)
            for r in range(c + 2, TILE):
                factor[r][c] = rest[r][c] * pivots[c][0] + rest[r][c + 1] * pivots[c][1]
                factor[r][c + 1] = rest[r][c] * pivots[c][1] + rest[r][c + 1] * pivots[c][2]
            for r in range(c + 2, TILE):
                for q in range(c + 2, r + 1):
                    rest[r][q] = rest[r][q] - (factor[r][c] * rest[q][c] + factor[r][c + 1] * rest[q][c + 1])
                for rows in up:
                    rows[r] = rows[r] - (factor[r][c] * rows[c] + factor[r][c + 1] * rows[c + 1])
            over_a = reciprocal(a)
            scaled[c] = lax.rsqrt(a) * up[1][c]
            scaled[c + 1] = lax.rsqrt(determinant * over_a) * (up[1][c + 1] - (b * over_a) * up[1][c])
        done.append(rows_of(scaled))
        if s == count - 1:
            break
        down = []
        for rows in up:
            solved = [None] * TILE
            for c in range(TILE - 2, -1, -2):
                p, q, t = pivots[c]
                one = p * rows[c] + q * rows[c + 1]
                two = q * rows[c] + t * rows[c + 1]
                for r in range(TILE - 1, c + 1, -1):
                    one = one - factor[r][c] * solved[r]
                    two = two - factor[r][c + 1] * solved[r]
                solved[c], solved[c + 1] = one, two
            down.append(solved)
        across = [spread(left[s + 1][:, TILE * s + c:TILE * s + c + 1]) for c in range(TILE)]
        for side, solved in zip((left, right), down):
            terms = [across[c] * solved[c] for c in range(TILE)]
            while len(terms) > 1:
                terms = [terms[i] + terms[i + 1] for i in range(0, len(terms), 2)]
            side[s + 1] = side[s + 1] - terms[0]
        if s + 2 < count:
            one, two, three = three_parts(left[s])
            stacked = jnp.concatenate([one, one, two, two, one, three], axis=0).astype(jnp.bfloat16)
            updates = []
            for solved in down:
                one, two, three = three_parts(rows_of(solved))
                updates.append(jnp.concatenate([one, two, one, two, three, one], axis=0).astype(jnp.bfloat16))
            update = lax.dot_general(
                stacked, jnp.concatenate(updates, axis=1), (((0,), (0,)), ((), ())),
                preferred_element_type=jnp.float32,
            )
            for t in range(s + 2, count):
                left[t] = left[t] - update[TILE * t:TILE * (t + 1), :BLOCK]
                right[t] = right[t] - update[TILE * t:TILE * (t + 1), BLOCK:]
    return jnp.concatenate(done, axis=0)


def inverse_kernel(place_ref, own_ref, other_ref, out_ref, rest, sums, lower):
    first = place_ref[0] == 0
    side = BLOCK // 2
    for z in range(8):
        for x in range(4):
            own, other = own_ref[4 * z + x], other_ref[4 * z + x]
            halves = [jnp.where(first, own, other), jnp.where(first, other, own)]
            middle = jnp.concatenate([half[16:16 + TILE, :side] for half in halves], axis=0)
            pieces = [halves[0][:16, :side], halves[0][:16, side:], middle, halves[1][:16, :side], halves[1][:16, side:]]
            for d, piece in enumerate(pieces):
                to = 64 * ((z + d) % 8) + 16 * x
                rest[to:to + 16, side * z:side * (z + 1)] = piece
    low = lax.broadcasted_iota(jnp.int32, (BLOCK, BLOCK), 0) >= side
    near = lax.broadcasted_iota(jnp.int32, (BLOCK, BLOCK), 1) < side
    for i in range(0, PANEL, BLOCK):
        for j in range(i, PANEL, BLOCK):
            here, there = rest[j:j + BLOCK, i:i + BLOCK], rest[i:i + BLOCK, j:j + BLOCK]
            turned = jnp.transpose(there)
            if j == i:
                rest[j:j + BLOCK, i:i + BLOCK] = jnp.where(low | near, here, turned)
            elif j == i + 2 * BLOCK:
                rest[j:j + BLOCK, i:i + BLOCK] = jnp.where(low & near, turned, here)
            elif j == i + 3 * BLOCK:
                rest[j:j + BLOCK, i:i + BLOCK] = turned
    slots = []
    for x in range(4):
        ahead = lax.rem(x - place_ref[1] + 4, 4)
        slots.append(jnp.where(ahead == 0, 0, jnp.where(ahead == 3, 1, ahead + 1)))

    def write(row, column, block):
        turned = None if block is None else jnp.transpose(block)
        for piece in range(0, BLOCK, 16):
            z, x = divmod((column + piece) // 16, 4)
            to = pl.multiple_of(slots[x] * 128 + 16 * z, 16)
            values = jnp.zeros((16, BLOCK), jnp.float32) if turned is None else turned[piece:piece + 16, :]
            out_ref[pl.ds(to, 16), row:row + BLOCK] = values

    starts = range(0, PANEL, BLOCK)
    at = {a: slice(a, a + BLOCK) for a in starts}
    beside = [functools.partial(write, a, k, None) for a in starts for k in starts if k > a]
    diagonal = rest[at[0], at[0]]
    for a in starts:
        inverse = factor_inverse(diagonal, beside)
        beside = []
        later = [i for i in starts if i > a]
        upper = {}
        if later:
            near = later[0]
            upper[near] = dot_parts(inverse, rest[at[near], at[a]], 1, 1)
            diagonal = rest[at[near], at[near]] - dot_parts(upper[near], upper[near], 0, 0)

        def finish(k, a=a, inverse=inverse):
            block = inverse if k == a else -dot_parts(inverse, sums[at[a], at[k]], 1, 0)
            lower[at[a], at[k]] = block
            write(a, k, block)

        def above(j, a=a, inverse=inverse, upper=upper):
            upper[j] = dot_parts(inverse, rest[at[j], at[a]], 1, 1)

        def update(i, j, upper=upper):
            rest[at[j], at[i]] = rest[at[j], at[i]] - dot_parts(upper[j], upper[i], 0, 0)

        def gather(i, k, a=a, upper=upper):
            term = dot_parts(upper[i], lower[at[a], at[k]], 0, 0)
            sums[at[i], at[k]] = term if k == a else sums[at[i], at[k]] + term

        beside += [functools.partial(above, j) for j in later[1:]]
        beside += [functools.partial(update, i, j) for i in later for j in later if j >= i and j > later[0]]
        beside += [functools.partial(finish, k) for k in starts if k <= a]
        beside += [functools.partial(gather, i, k) for i in later for k in starts if k <= a]
    for step in beside:
        step()


def inverse_factor(place, own, other):
    shape = (PANEL, PANEL)
    return pl.pallas_call(
        inverse_kernel,
        out_shape=jax.ShapeDtypeStruct(shape, jnp.float32),
        in_specs=[pl.BlockSpec(memory_space=pltpu.SMEM)] + [pl.BlockSpec(memory_space=pltpu.VMEM)] * 2,
        out_specs=pl.BlockSpec(memory_space=pltpu.VMEM),
        scratch_shapes=[pltpu.VMEM(shape, jnp.float32)] * 3,
        compiler_params=pltpu.CompilerParams(vmem_limit_bytes=16 << 20),
        cost_estimate=pl.CostEstimate(flops=4 * PANEL ** 3, bytes_accessed=8 * PANEL ** 2, transcendentals=PANEL),
        name="inverse_factor",
    )(place, own, other)


def prepare_kernel(counts_ref, barrier_ref, border_ref, along_ref, beside_ref, other_ref, columns, arrived, moved):
    capacity = barrier_ref.shape[1]
    copies = [
        pltpu.make_async_copy(border_ref.at[s, :, pl.ds(0, 128)], columns.at[s], arrived.at[s]) for s in range(2)
    ]
    for copy in copies:
        copy.start()
    other = pltpu.make_async_copy(border_ref.at[1 - lax.axis_index("core")], other_ref, moved)
    other.start()
    position = lax.broadcasted_iota(jnp.int32, (1, capacity), 1)
    for s in range(2):
        weights = jnp.where(position < counts_ref[s], 1.0 / barrier_ref[s:s + 1, :], 0.0)
        copies[s].wait()
        tiles = [jnp.transpose(columns[s, a:a + 128, :])[:TILE, :] for a in range(0, capacity, 128)]
        panel = jnp.concatenate(tiles, axis=1)
        weighted = panel * weights
        for z in range(8):
            along_ref[2 * z + s] = weighted
        beside_ref[s] = panel
    other.wait()


def prepare(row_counts, barrier, border):
    capacity = border.shape[1]
    vmem = pl.BlockSpec(memory_space=pltpu.VMEM)
    return pl.pallas_call(
        prepare_kernel,
        out_shape=(
            jax.ShapeDtypeStruct((16, TILE, capacity), jnp.float32),
            jax.ShapeDtypeStruct((2, TILE, capacity), jnp.float32),
            jax.ShapeDtypeStruct(border.shape[1:], jnp.float32),
        ),
        in_specs=[pl.BlockSpec(memory_space=pltpu.SMEM), vmem, pl.BlockSpec(memory_space=pltpu.HBM)],
        out_specs=(vmem, vmem, vmem),
        scratch_shapes=[
            pltpu.VMEM((2, capacity, 128), jnp.float32),
            pltpu.SemaphoreType.DMA((2,)),
            pltpu.SemaphoreType.DMA(()),
        ],
        compiler_params=pltpu.CompilerParams(vmem_limit_bytes=60 << 20),
        name="prepare",
    )(row_counts, barrier, border)


def block_kernel(along_ref, beside_ref, out_ref, part_ref):
    along = along_ref[...].reshape(16 * TILE, -1)
    scenario = pl.ds(lax.axis_index("core"), 1)
    beside = jnp.concatenate([beside_ref[p, scenario, :, :].reshape(TILE, -1) for p in range(8)], axis=0)
    part_ref[...] = dot_parts(along, beside, 1, 1)
    z = lax.axis_index("z")
    rows = [part_ref[pl.ds(pl.multiple_of(lax.rem(z + d, 8) * 16, 16), 16), :] for d in range(5)]
    packed = [
        jnp.concatenate(
            [
                jnp.concatenate([rows[3 * c], rows[3 * c + 1]], axis=1),
                jnp.concatenate([rows[2][TILE * c:TILE * (c + 1)]] * 2, axis=1),
            ],
            axis=0,
        )
        for c in range(2)
    ]
    for y in range(8):
        for c in range(2):
            out_ref[2 * y + c] = packed[c]


def block_part(along, beside):
    vmem = pl.BlockSpec(memory_space=pltpu.VMEM)
    return pl.pallas_call(
        block_kernel,
        out_shape=jax.ShapeDtypeStruct((16, 3 * TILE, 16 * TILE), jnp.float32),
        in_specs=[vmem, vmem],
        out_specs=vmem,
        scratch_shapes=[pltpu.VMEM((16 * TILE, 8 * TILE), jnp.float32)],
        compiler_params=pltpu.CompilerParams(vmem_limit_bytes=16 << 20),
        name="block_part",
    )(along, beside)


def product_kernel(columns_ref, *refs):
    *panel_refs, out_ref = refs
    panel = jnp.concatenate([ref[...] for ref in panel_refs], axis=0)
    columns, columns_low = two_parts(columns_ref[...])
    panel, panel_low = two_parts(panel)
    total = jnp.dot(panel, columns, preferred_element_type=jnp.float32)
    total = total + jnp.dot(panel, columns_low, preferred_element_type=jnp.float32)
    total = total + jnp.dot(panel_low, columns, preferred_element_type=jnp.float32)
    out_ref[:, out_ref.shape[1] - total.shape[0]:] = jnp.transpose(total)


def further_kernel(columns_ref, panel_ref, before_ref, out_ref):
    out_ref[:, :before_ref.shape[1]] = before_ref[...]
    product_kernel(columns_ref, panel_ref, out_ref)


def product(columns, panels, before=None):
    rows, width = columns.shape
    fresh = sum(panel.shape[0] for panel in panels)
    done = () if before is None else (before,)
    vmem = pl.BlockSpec(memory_space=pltpu.VMEM)
    return pl.pallas_call(
        further_kernel if done else product_kernel,
        out_shape=jax.ShapeDtypeStruct((width, fresh + sum(b.shape[1] for b in done)), jnp.float32),
        in_specs=[vmem] * (1 + len(panels) + len(done)),
        out_specs=vmem,
        compiler_params=pltpu.CompilerParams(vmem_limit_bytes=32 << 20),
        cost_estimate=pl.CostEstimate(
            flops=6 * rows * width * fresh, bytes_accessed=4 * rows * (width + fresh), transcendentals=0
        ),
        name="further" if done else "product",
    )(columns, *panels, *done)


def exchange(array, axes):
    return lax.all_to_all(array, axes, split_axis=0, concat_axis=0, tiled=True)


def body(border, barrier, row_counts):
    capacity = border.shape[1]
    own_cols = border.shape[2]
    n_scen = lax.axis_size("scen")
    rows_owned = own_cols // n_scen
    core = lax.axis_index("core")
    place = jnp.stack([core, lax.axis_index("x")])

    to_along, to_beside, to_other = prepare(row_counts, barrier, border)
    along = exchange(to_along, ("z", "core"))
    beside = lax.all_gather(to_beside, ("x", "core"), axis=0, tiled=False)
    along, beside = lax.optimization_barrier((along, beside))

    shard = along.reshape(16 * TILE, capacity)
    behind = lax.ppermute(shard, "x", AHEAD)
    ahead = lax.ppermute(shard, "x", BEHIND)

    piece = block_part(along, beside)
    parts = exchange(piece, ("scen", "core"))
    behind, to_other = lax.optimization_barrier((behind, to_other))
    other = lax.ppermute(to_other, "core", SWAP)
    _, passed_on = lax.optimization_barrier((piece, jnp.where(core == 0, behind, ahead)))
    onward = lax.ppermute(passed_on, ("x", "core"), ONWARD)
    parts, _ = lax.optimization_barrier((parts, passed_on))
    summed = jnp.sum(parts, axis=0)
    copies = jnp.broadcast_to(summed, (32,) + summed.shape)
    own_half = exchange(copies, ("z", "x"))
    other_half = lax.ppermute(own_half, "core", SWAP)
    inverse = inverse_factor(place, own_half, other_half)

    mine = lax.dynamic_index_in_dim(border, core, 0, keepdims=False)
    schur_other = product(other, (shard, behind, ahead))
    schur_mine = product(mine, (shard, behind, ahead))
    onward, schur_other, schur_mine = lax.optimization_barrier((onward, schur_other, schur_mine))
    schur_other = product(other, (onward,), schur_other)
    schur_mine = product(mine, (onward,), schur_mine)
    schur_part = schur_mine + lax.ppermute(schur_other, "core", SWAP)
    owned = jnp.sum(exchange(schur_part.reshape(n_scen, rows_owned, PANEL), "scen"), axis=0)
    solved = dot(owned, inverse, 1, 0)
    return solved.reshape(1, 1, rows_owned, PANEL)


def solution(mesh):
    inner = Mesh(mesh.devices.reshape(mesh.shape["scen"], 8, 4, 2), ("scen",) + COL)
    placed = (P("scen", None, COL), P("scen", None), P("scen"))
    return jax.shard_map(
        body, mesh=inner, in_specs=placed, out_specs=P(COL, "scen", None, None), check_vma=False
    )
```
